512 devices in a mesh: wide: 64 (over z, x), narrow: 8 (over y, core).
Axes of the slice: x: 4, y: 4, z: 16, core: 2. Of those that a mesh axis runs over, the one named last changes fastest.
Arguments:
- fine_state: bfloat16 [524288, 256], P(('wide', 'narrow')), may hold values from -6 to 6
- l2_state: bfloat16 [16384, 256], P('wide'), may hold values from -3 to 3
- l3_state: bfloat16 [4096, 256], replicated, may hold values from -3 to 3
- boundary: int32 [8192], P(('wide', 'narrow')), may hold values from 0 to 1023
- senders: int32 [1048576], P(('wide', 'narrow')), may hold values from 0 to 1407
- receivers: int32 [1048576], P(('wide', 'narrow')), may hold values from 0 to 1024
- up_parent: int32 [524288], P(('wide', 'narrow')), may hold values from 0 to 255
- l2_parent: int32 [16384], P('wide'), may hold values from 0 to 4095, as said below
- msg_in: bfloat16 [512, 256], replicated, may hold values from -0.25 to 0.25
- msg_out: bfloat16 [256, 256], replicated, may hold values from -0.375 to 0.375
- fine_gain: float32 [256], replicated, may hold values from 0.1 to 1.9
- up_weight: bfloat16 [256, 256], replicated, may hold values from -0.375 to 0.375
- l2_gain: float32 [256], replicated, may hold values from 0.1 to 1.9
- l3_gain: float32 [256], replicated, may hold values from 0.1 to 1.9
- l3_w1: bfloat16 [256, 256], replicated, may hold values from -0.375 to 0.375
- l3_w2: bfloat16 [256, 256], replicated, may hold values from -0.375 to 0.375
- down_weight: bfloat16 [256, 256], replicated, may hold values from -0.375 to 0.375
- fine_down: bfloat16 [256, 256], replicated, may hold values from -0.375 to 0.375
Outputs:
- fine_out: bfloat16 [524288, 256], P(('wide', 'narrow'))
- l2_down: bfloat16 [16384, 256], P('wide')
The draws below stay inside these ranges and needn't reach their ends.
Inputs may be any that keep to these rules, and one draw needn't show every extreme that they name: `boundary`: local fine node indices. `senders`: index into the device's pool of 1408 rows. `receivers`: 1024 marks a padding slot. `up_parent`: index among the 256 level-2 nodes of the device's patch. `l2_parent`: the parent of a level-2 node of patch w lies in one of the level-3 blocks w - 1, w, w + 1 (modulo 64), block b being nodes b * 64 to b * 64 + 63.
All inputs are finite; a program needn't handle non-finite values.
Results may differ from the reference program's by a relative error of at most 0.014.
Values may be sent and summed in bfloat16 or wider, within the bound.
No kernel may reach another device: no remote copies, remote signals or barrier semaphores. Data moves between devices by JAX's collectives and lax.ppermute only.
A program may use at most 64 MiB of HBM per device.

```python
import jax
import jax.numpy as jnp
from jax import lax

D = 256
NODE_DEV = 1024
EDGE_DEV = 2048
BND = 16
L2_DEV = 256
L3_DEV = 64
FINE_N = 524288
FINE_E = 1048576
BNDS = 8192
L2_N = 16384
L3_N = 4096
POOL = 1408
N_WIDE = 64
N_NARROW = 8


def draw_l2_parent(key, part):
    key = jax.random.fold_in(key, 11)
    first, second = jax.random.split(key)
    patch_of = jnp.arange(L2_N, dtype=jnp.int32) // L2_DEV
    pick = jax.random.randint(first, (L2_N,), 0, 4, dtype=jnp.int32)
    offset = jnp.where(pick == 0, -1, jnp.where(pick == 1, 1, 0)).astype(jnp.int32)
    block = (patch_of + offset + N_WIDE) % N_WIDE
    inner = jax.random.randint(second, (L2_N,), 0, L3_DEV, dtype=jnp.int32)
    return (block * L3_DEV + inner).astype(jnp.int32)


def set_ends(array, rng, low, high):
    dims = array.shape
    spot = [jax.random.randint(jax.random.fold_in(rng, axis), (), 0, dims[axis]) for axis in range(len(dims))]
    array = array.at[tuple(spot)].set(low)
    longest = dims.index(max(dims))
    spot[longest] = (spot[longest] + 1) % dims[longest]
    return array.at[tuple(spot)].set(high)


def block_scale(rng, shape, shards, least, largest):
    loudness = 1.0
    for axis_at, shards_of in shards:
        draws = jax.random.uniform(jax.random.fold_in(jax.random.fold_in(rng, 6), axis_at), (shards_of,), jnp.float32, least / len(shards), largest / len(shards))
        loudness = loudness * jnp.repeat(jnp.exp(draws), shape[axis_at] // shards_of).reshape((-1,) + (1,) * (len(shape) - 1 - axis_at))
    return loudness


def bell_draw(key, extent, spread, bound, cuts=(), kind=jnp.bfloat16):
    drawn = jax.random.normal(key, extent, jnp.float32) * spread
    if len(cuts) > 0:
        drawn = block_scale(key, extent, cuts, -0.22, 0.18) * drawn
    return jnp.clip(drawn, min=-bound, max=bound).astype(kind)


def setup_inputs(seed: int = 0) -> dict:
    splits = jax.random.split(jax.random.key(seed), 19)
    return {
        "fine_state": bell_draw(splits[0], (FINE_N, D), 1.0, 6.0, ((0, 512),)),
        "l2_state": bell_draw(splits[1], (L2_N, D), 0.5, 3.0, ((0, 64),)),
        "l3_state": bell_draw(splits[2], (L3_N, D), 0.5, 3.0),
        "boundary": set_ends(jax.random.randint(splits[3], (BNDS,), 0, NODE_DEV), jax.random.fold_in(splits[3], 1), 0, NODE_DEV - 1).astype(jnp.int32),
        "senders": set_ends(jax.random.randint(splits[4], (FINE_E,), 0, POOL), jax.random.fold_in(splits[4], 1), 0, POOL - 1).astype(jnp.int32),
        "receivers": set_ends(jax.random.randint(splits[5], (FINE_E,), 0, NODE_DEV + 1), jax.random.fold_in(splits[5], 1), 0, NODE_DEV).astype(jnp.int32),
        "up_parent": set_ends(jax.random.randint(splits[6], (FINE_N,), 0, L2_DEV), jax.random.fold_in(splits[6], 1), 0, L2_DEV - 1).astype(jnp.int32),
        "l2_parent": draw_l2_parent(jax.random.fold_in(splits[18], 71), 0),
        "msg_in": bell_draw(splits[8], (2 * D, D), (2 * D) ** -0.5, 0.25),
        "msg_out": bell_draw(splits[9], (D, D), D ** -0.5, 0.375),
        "fine_gain": jnp.clip(1.0 + 0.18 * jax.random.normal(splits[10], (D,), jnp.float32), 0.1, 1.9),
        "up_weight": bell_draw(splits[11], (D, D), D ** -0.5, 0.375),
        "l2_gain": jnp.clip(1.0 + 0.18 * jax.random.normal(splits[12], (D,), jnp.float32), 0.1, 1.9),
        "l3_gain": jnp.clip(1.0 + 0.18 * jax.random.normal(splits[13], (D,), jnp.float32), 0.1, 1.9),
        "l3_w1": bell_draw(splits[14], (D, D), D ** -0.5, 0.375),
        "l3_w2": bell_draw(splits[15], (D, D), D ** -0.5, 0.375),
        "down_weight": bell_draw(splits[16], (D, D), D ** -0.5, 0.375),
        "fine_down": bell_draw(splits[17], (D, D), D ** -0.5, 0.375),
    }


def rms_scale(values, gain):
    return values * lax.rsqrt(lax.optimization_barrier(jnp.mean(values * values, axis=-1, keepdims=True)) + 1e-05) * gain

def reference(fine_state, l2_state, l3_state, boundary, senders, receivers, up_parent, l2_parent, msg_in, msg_out, fine_gain, up_weight, l2_gain, l3_gain, l3_w1, l3_w2, down_weight, fine_down):
    devs = N_WIDE * N_NARROW
    nodes = fine_state.reshape(devs, NODE_DEV, D)
    bidx = boundary.reshape(devs, BND)
    exported = jnp.take_along_axis(nodes, bidx[:, :, None], axis=1)
    patch = exported.reshape(N_WIDE, N_NARROW * BND, D)
    beside_all = jnp.concatenate([jnp.roll(patch, 1, 0), patch, jnp.roll(patch, -1, 0)], axis=1)
    around_dev = jnp.repeat(beside_all, N_NARROW, axis=0)
    send = senders.reshape(devs, EDGE_DEV)
    recv = receivers.reshape(devs, EDGE_DEV)

    def fine_one(items):
        node, rest, sidx, ridx = items
        pool = jnp.concatenate([node, rest], axis=0)
        sender_rows = jnp.take(pool, sidx, axis=0)
        receiver_rows = jnp.take(node, jnp.minimum(ridx, NODE_DEV - 1), axis=0)
        joined = jnp.concatenate([sender_rows, receiver_rows], axis=1)
        edge_hidden = jax.nn.silu(jnp.dot(joined, msg_in, preferred_element_type=jnp.float32)).astype(jnp.bfloat16)
        message = jnp.dot(edge_hidden, msg_out, preferred_element_type=jnp.float32).astype(jnp.bfloat16)
        agg = jax.ops.segment_sum(message.astype(jnp.float32), ridx, num_segments=NODE_DEV + 1)[:NODE_DEV]
        return (node.astype(jnp.float32) + rms_scale(agg, fine_gain)).astype(jnp.bfloat16)
    fine_mid = lax.map(fine_one, (nodes, around_dev, send, recv)).reshape(devs * NODE_DEV, D)
    up_term = jnp.dot(fine_mid, up_weight, preferred_element_type=jnp.float32).astype(jnp.bfloat16)
    owner = (jnp.arange(devs, dtype=jnp.int32) // N_NARROW)[:, None] * L2_DEV
    gidx = (owner + up_parent.reshape(devs, NODE_DEV)).reshape(-1).astype(jnp.int32)
    l2_sum = jax.ops.segment_sum(up_term.astype(jnp.float32), gidx, num_segments=L2_N)
    l2_mid = (l2_state.astype(jnp.float32) + rms_scale(l2_sum, l2_gain)).astype(jnp.bfloat16)
    l3_sum = jax.ops.segment_sum(l2_mid.astype(jnp.float32), l2_parent, num_segments=L3_N)
    l3_mid = (l3_state.astype(jnp.float32) + rms_scale(l3_sum, l3_gain)).astype(jnp.bfloat16)
    l3_hidden = jax.nn.silu(jnp.dot(l3_mid, l3_w1, preferred_element_type=jnp.float32)).astype(jnp.bfloat16)
    l3_new = (l3_mid.astype(jnp.float32) + jnp.dot(l3_hidden, l3_w2, preferred_element_type=jnp.float32)).astype(jnp.bfloat16)
    l2_down = (l2_mid.astype(jnp.float32) + jnp.dot(jnp.take(l3_new, l2_parent, axis=0), down_weight, preferred_element_type=jnp.float32)).astype(jnp.bfloat16)
    fine_out = (fine_mid.astype(jnp.float32) + jnp.dot(jnp.take(l2_down, gidx, axis=0), fine_down, preferred_element_type=jnp.float32)).astype(jnp.bfloat16)
    return (fine_out, l2_down)
```

```python
import functools

import jax
import jax.numpy as jnp
from jax import lax
from jax.experimental import pallas as pl
from jax.experimental.pallas import tpu as pltpu
from jax.sharding import PartitionSpec as P

F32 = jnp.float32
BF16 = jnp.bfloat16
LANES = 128
EDGE_BLOCK = 512


def dot(a, b):
    return jnp.dot(a, b, preferred_element_type=F32)


def rms_scale(values, gain):
    return values * lax.rsqrt(jnp.mean(values * values, axis=-1, keepdims=True) + 1e-05) * gain


def silu(x):
    half = 0.5 * x
    return half + half * jnp.tanh(half)


def column_parts(index):
    low = (index & (LANES - 1)).astype(F32)
    high = (index >> 7).astype(F32)
    return low.T, high.T


def lane_select(low_col, high_col):
    lane = lax.broadcasted_iota(jnp.int32, (LANES, LANES), 1).astype(F32)
    low = jnp.broadcast_to(low_col, (LANES, LANES))
    hot = jnp.where(low == lane, 1.0, 0.0).astype(BF16)
    high = jnp.broadcast_to(high_col, (LANES, LANES)).astype(BF16)
    return hot, high


def row_select(index_row):
    sub = lax.broadcasted_iota(jnp.int32, (LANES, LANES), 0)
    hot = jnp.where((index_row & (LANES - 1)) == sub, 1.0, 0.0).astype(BF16)
    high = jnp.broadcast_to((index_row >> 7).astype(F32), (LANES, LANES)).astype(BF16)
    return hot, high


def pick(hot, high, tile):
    return jnp.where(high == jnp.asarray(tile, BF16), hot, jnp.zeros_like(hot))


def fetch(pairs, sems):
    copies = [pltpu.make_async_copy(a, b, sems.at[k]) for k, (a, b) in enumerate(pairs)]
    for copy in copies:
        copy.start()
    for copy in copies:
        copy.wait()


def gathered(index_ref, proj, hot, out_ref, before_ref=None):
    tiles = proj.shape[0] // LANES
    low, high = column_parts(index_ref[...])
    for block in range(out_ref.shape[0] // EDGE_BLOCK):
        for part in range(EDGE_BLOCK // LANES):
            j = block * (EDGE_BLOCK // LANES) + part
            span = slice(j * LANES, (j + 1) * LANES)
            hot_j, high_j = lane_select(low[:, j : j + 1], high[:, j : j + 1])
            for t in range(tiles):
                hot[span, t * LANES : (t + 1) * LANES] = pick(hot_j, high_j, t)
        span = slice(block * EDGE_BLOCK, (block + 1) * EDGE_BLOCK)
        rows = dot(hot[span], proj[...])
        out_ref[span] = rows if before_ref is None else rows + before_ref[span]


def receiver_kernel(fs_hbm, recv_hbm, w_in_hbm, pre_ref, fs, recv, w_in, proj, hot, sems):
    width = fs.shape[1]
    fetch([(fs_hbm, fs), (recv_hbm, recv), (w_in_hbm.at[pl.ds(width, width)], w_in)], sems)
    proj[...] = dot(fs[...], w_in[...]).astype(BF16)
    gathered(recv, proj, hot, pre_ref)


def sender_kernel(
    before_ref, fs_hbm, send_hbm, w_in_hbm, l3_hbm, pre_ref, l3_rows_ref, fs, send, w_in, proj, hot, sems
):
    width = fs.shape[1]
    wide = lax.axis_index("wide")
    count = lax.axis_size("wide")
    rows = l3_rows_ref.shape[0] // 3
    pairs = [(fs_hbm, fs), (send_hbm, send), (w_in_hbm.at[pl.ds(0, width)], w_in)]
    for k in range(3):
        block = lax.rem(wide + (k + count - 1), count)
        pairs.append(
            (
                l3_hbm.at[pl.ds(pl.multiple_of(block * rows, rows), rows)],
                l3_rows_ref.at[pl.ds(k * rows, rows)],
            )
        )
    fetch(pairs, sems)
    proj[...] = dot(fs[...], w_in[...]).astype(BF16)
    gathered(send, proj, hot, pre_ref, before_ref)


def fine_kernel(
    pre_ref, around_ref, fs_ref, send_ref, recv_ref, par_ref, w_in_ref, w_out_ref, gain_ref,
    mid_ref, keep_ref, give_ref, hidden, hot, inc, sums,
):
    nodes, width = fs_ref.shape
    edges = pre_ref.shape[0]
    tiles = nodes // LANES
    extra = around_ref.shape[0] // LANES
    proj = dot(around_ref[...], w_in_ref[:width]).astype(BF16)
    send_low, send_high = column_parts(send_ref[...])
    for block in range(edges // EDGE_BLOCK):
        for part in range(EDGE_BLOCK // LANES):
            j = block * (EDGE_BLOCK // LANES) + part
            span = slice(j * LANES, (j + 1) * LANES)
            hot_s, high_s = lane_select(send_low[:, j : j + 1], send_high[:, j : j + 1])
            for t in range(extra):
                hot[span, t * LANES : (t + 1) * LANES] = pick(hot_s, high_s, tiles + t)
            hot_r, high_r = row_select(recv_ref[j : j + 1])
            for t in range(tiles):
                inc[t * LANES : (t + 1) * LANES, span] = pick(hot_r, high_r, t)
        span = slice(block * EDGE_BLOCK, (block + 1) * EDGE_BLOCK)
        hidden[span] = silu(pre_ref[span] + dot(hot[span], proj)).astype(BF16)
    for block in range(nodes // EDGE_BLOCK):
        span = slice(block * EDGE_BLOCK, (block + 1) * EDGE_BLOCK)
        agg = dot(dot(inc[span], hidden[...]).astype(BF16), w_out_ref[...])
        mid_ref[span] = (fs_ref[span].astype(F32) + rms_scale(agg, gain_ref[...])).astype(BF16)
    total = jnp.zeros(sums.shape, F32)
    for j in range(tiles):
        hot_p, high_p = row_select(par_ref[j : j + 1])
        upper = jnp.concatenate([pick(hot_p, high_p, t) for t in range(sums.shape[0] // LANES)], axis=0)
        total = total + dot(upper, mid_ref[j * LANES : (j + 1) * LANES])
    sums[...] = total
    half = keep_ref.shape[0]
    core = lax.rem(lax.axis_index("narrow"), 2)
    keep_ref[...] = sums[pl.ds(pl.multiple_of(core * half, half), half)]
    give_ref[...] = sums[pl.ds(pl.multiple_of((1 - core) * half, half), half)].astype(BF16)


def add_kernel(a_ref, b_ref, out_ref):
    out_ref[...] = (a_ref[...].astype(F32) + b_ref[...].astype(F32)).astype(BF16)


def level_two_kernel(a_ref, b_ref, state_ref, w_up_ref, gain_ref, out_ref):
    rows = out_ref.shape[0]
    core = lax.rem(lax.axis_index("narrow"), 2)
    total = a_ref[...].astype(F32) + b_ref[...].astype(F32)
    level = dot(total.astype(BF16), w_up_ref[...])
    state = state_ref[pl.ds(pl.multiple_of(core * rows, rows), rows)].astype(F32)
    out_ref[...] = (state + rms_scale(level, gain_ref[...])).astype(BF16)


def coarse_parent(parent_ref, rows, level_three):
    start = (lax.axis_index("wide") - 1) * rows
    local = (parent_ref[...] - start) & (level_three - 1)
    sub = lax.broadcasted_iota(jnp.int32, (3 * rows, LANES), 0)
    return jnp.concatenate(
        [jnp.where(local[j : j + 1] == sub, 1.0, 0.0) for j in range(parent_ref.shape[0])], axis=1
    )


def window_kernel(level_three, mine_ref, other_ref, parent_ref, own_ref, piece_ref, mid_ref):
    half = mine_ref.shape[0]
    rows = piece_ref.shape[0]
    narrow = lax.axis_index("narrow")
    core = lax.rem(narrow, 2)
    chip = narrow // 2
    mid_ref[pl.ds(pl.multiple_of(core * half, half), half)] = mine_ref[...]
    mid_ref[pl.ds(pl.multiple_of((1 - core) * half, half), half)] = other_ref[...]
    upper = coarse_parent(parent_ref, rows, level_three).astype(BF16)
    own_ref[...] = dot(upper, mid_ref[...])
    block = jnp.where(chip == 0, 1 + core, jnp.where(chip == 1, core, jnp.where(chip == 2, 2, 0)))
    piece_ref[...] = own_ref[pl.ds(pl.multiple_of(block * rows, rows), rows)].astype(BF16)


def down_kernel(
    level_three, own_ref, pieces_ref, l3_rows_ref, gain_ref,
    w1_ref, w2_ref, w_down_ref, w_fine_ref, parent_ref, mid_ref, par_ref, fine_ref,
    fine_out_ref, down_ref,
):
    rows = pieces_ref.shape[1]
    own = own_ref[...]
    piece = [pieces_ref[k].astype(F32) for k in (0, 1, 2, 3, 4, 6)]
    total = jnp.concatenate(
        [
            own[:rows] + piece[0] + piece[4],
            own[rows : 2 * rows] + piece[1] + piece[2],
            own[2 * rows :] + piece[3] + piece[5],
        ],
        axis=0,
    )
    mid3 = (l3_rows_ref[...].astype(F32) + rms_scale(total, gain_ref[...])).astype(BF16)
    hidden = silu(dot(mid3, w1_ref[...])).astype(BF16)
    new = (mid3.astype(F32) + dot(hidden, w2_ref[...])).astype(BF16)
    lower = coarse_parent(parent_ref, rows, level_three).T.astype(BF16)
    picked = dot(lower, new).astype(BF16)
    down = (mid_ref[...].astype(F32) + dot(picked, w_down_ref[...])).astype(BF16)
    down_ref[...] = down
    fine = dot(down, w_fine_ref[...]).astype(BF16)
    par_low, par_high = column_parts(par_ref[...])
    for j in range(par_ref.shape[0]):
        hot, high = lane_select(par_low[:, j : j + 1], par_high[:, j : j + 1])
        lower = jnp.concatenate([pick(hot, high, t) for t in range(fine.shape[0] // LANES)], axis=1)
        span = slice(j * LANES, (j + 1) * LANES)
        fine_out_ref[span] = (fine_ref[span].astype(F32) + dot(lower, fine)).astype(BF16)


def passed_along(value, steps):
    count = lax.axis_size("wide")
    return lax.ppermute(value, "wide", [(k, (k + steps) % count) for k in range(count)])


def swapped(value, partner):
    count = lax.axis_size("narrow")
    return lax.ppermute(value, "narrow", [(k, partner(k)) for k in range(count)])


def served(value):
    wide, narrow = lax.axis_size("wide"), lax.axis_size("narrow")
    steps = (1, -1, 2, -2)
    pairs = [
        (w * narrow + n, (w + steps[n // 2]) % wide * narrow + n)
        for w in range(wide)
        for n in range(narrow)
    ]
    return lax.ppermute(value, ("wide", "narrow"), pairs)


def call(kernel, out, scratch=(), vmem=48, hbm=(), nargs=0, flops=0, moved=0):
    specs = [
        pl.BlockSpec(memory_space=pltpu.HBM if k in hbm else pltpu.VMEM) for k in range(nargs)
    ]
    outs = [jax.ShapeDtypeStruct(shape, dtype) for shape, dtype in out]
    return pl.pallas_call(
        kernel,
        out_shape=outs,
        in_specs=specs,
        out_specs=[pl.BlockSpec(memory_space=pltpu.VMEM) for _ in outs],
        scratch_shapes=list(scratch),
        compiler_params=pltpu.CompilerParams(vmem_limit_bytes=vmem * 2**20),
        cost_estimate=pl.CostEstimate(flops=flops, bytes_accessed=moved, transcendentals=0),
    )


def body(
    fine_state, l2_state, l3_state, boundary, senders, receivers, up_parent, l2_parent, msg_in,
    msg_out, fine_gain, up_weight, l2_gain, l3_gain, l3_w1, l3_w2, down_weight, fine_down,
):
    nodes, width = fine_state.shape
    edges = senders.shape[0]
    level_two = l2_state.shape[0]
    level_three = l3_state.shape[0]
    rows = level_three // lax.axis_size("wide")
    n_narrow = lax.axis_size("narrow")
    send = senders.reshape(-1, LANES)
    recv = receivers.reshape(-1, LANES)
    par = up_parent.reshape(-1, LANES)
    parent = l2_parent.reshape(-1, LANES)
    fine_gain, l2_gain, l3_gain = (g.reshape(1, width) for g in (fine_gain, l2_gain, l3_gain))

    hot = (boundary[:, None] == jnp.arange(nodes, dtype=jnp.int32)[None, :]).astype(BF16)
    exported = dot(hot, fine_state).astype(BF16)
    behind, ahead = passed_along(exported, 1), passed_along(exported, -1)
    scratch = [
        pltpu.VMEM((nodes, width), BF16),
        pltpu.VMEM(send.shape, jnp.int32),
        pltpu.VMEM((width, width), BF16),
        pltpu.VMEM((nodes, width), BF16),
        pltpu.VMEM((edges, nodes), BF16),
        pltpu.SemaphoreType.DMA((6,)),
    ]
    (pre_recv,) = call(
        receiver_kernel, [((edges, width), F32)], scratch, hbm=(0, 1, 2), nargs=3,
        flops=2_000_000_000, moved=2_000_000,
    )(fine_state, recv, msg_in)
    behind, ahead, pre_recv = lax.optimization_barrier((behind, ahead, pre_recv))
    window = jnp.concatenate([behind, exported, ahead], axis=0)
    window = jnp.broadcast_to(window[None], (n_narrow,) + window.shape)
    window = lax.all_to_all(window, "narrow", 0, 0, tiled=True)
    bnd = boundary.shape[0]
    around = window.reshape(n_narrow, 3, bnd, width).transpose(1, 0, 2, 3).reshape(-1, width)

    pre, l3_rows = call(
        sender_kernel, [((edges, width), F32), ((3 * rows, width), BF16)], scratch,
        hbm=(1, 2, 3, 4), nargs=5, flops=2_000_000_000, moved=2_000_000,
    )(pre_recv, fine_state, send, msg_in, l3_state)

    half = level_two // 2
    fine_mid, keep, give = call(
        fine_kernel,
        [((nodes, width), BF16), ((half, width), F32), ((half, width), BF16)],
        [
            pltpu.VMEM((edges, width), BF16),
            pltpu.VMEM((edges, around.shape[0]), BF16),
            pltpu.VMEM((nodes, edges), BF16),
            pltpu.VMEM((level_two, width), F32),
        ],
        nargs=9, flops=3_000_000_000, moved=4_000_000,
    )(pre, around, fine_state, send, recv, par, msg_in, msg_out, fine_gain)

    half_out = [((half, width), BF16)]
    (chip_sum,) = call(add_kernel, half_out, nargs=2)(keep, swapped(give, lambda k: k ^ 1))
    (pair_sum,) = call(add_kernel, half_out, nargs=2)(chip_sum, swapped(chip_sum, lambda k: k ^ 2))
    (half_mid,) = call(level_two_kernel, half_out, nargs=5)(
        pair_sum, swapped(pair_sum, lambda k: (n_narrow // 2 - 1 - k // 2) * 2 + k % 2),
        l2_state, up_weight, l2_gain,
    )
    own, piece, l2_mid = call(
        functools.partial(window_kernel, level_three),
        [((3 * rows, width), F32), ((rows, width), BF16), ((level_two, width), BF16)],
        nargs=3,
    )(half_mid, swapped(half_mid, lambda k: k ^ 1), parent)
    piece = served(piece)
    pieces = jnp.broadcast_to(piece[None], (n_narrow,) + piece.shape)
    pieces = lax.all_to_all(pieces, "narrow", 0, 0, tiled=True)

    fine_out, l2_down = call(
        functools.partial(down_kernel, level_three),
        [((nodes, width), BF16), ((level_two, width), BF16)],
        nargs=12,
    )(
        own, pieces, l3_rows, l3_gain, l3_w1, l3_w2, down_weight, fine_down,
        parent, l2_mid, par, fine_mid,
    )
    return (fine_out, l2_down)


def solution(mesh):
    both = P(("wide", "narrow"))
    return jax.shard_map(
        body,
        mesh=mesh,
        in_specs=(
            P(("wide", "narrow"), None),
            P("wide", None),
            P(),
            both,
            both,
            both,
            both,
            P("wide"),
        )
        + (P(),) * 10,
        out_specs=(P(("wide", "narrow"), None), P("wide", None)),
        check_vma=False,
    )
```

```python
import functools

import jax
import jax.numpy as jnp
from jax import lax
from jax.experimental import pallas as pl
from jax.experimental.pallas import tpu as pltpu
from jax.sharding import PartitionSpec as P

F32 = jnp.float32
BF16 = jnp.bfloat16
LANES = 128
EDGE_BLOCK = 512


def dot(a, b):
    return jnp.dot(a, b, preferred_element_type=F32)


def rms_scale(values, gain):
    return values * lax.rsqrt(jnp.mean(values * values, axis=-1, keepdims=True) + 1e-05) * gain


def silu(x):
    half = 0.5 * x
    return half + half * jnp.tanh(half)


def column_parts(index):
    low = (index & (LANES - 1)).astype(F32)
    high = (index >> 7).astype(F32)
    return low.T, high.T


def lane_select(low_col, high_col):
    lane = lax.broadcasted_iota(jnp.int32, (LANES, LANES), 1).astype(F32)
    low = jnp.broadcast_to(low_col, (LANES, LANES))
    hot = jnp.where(low == lane, 1.0, 0.0).astype(BF16)
    high = jnp.broadcast_to(high_col, (LANES, LANES)).astype(BF16)
    return hot, high


def row_select(index_row):
    sub = lax.broadcasted_iota(jnp.int32, (LANES, LANES), 0)
    hot = jnp.where((index_row & (LANES - 1)) == sub, 1.0, 0.0).astype(BF16)
    high = jnp.broadcast_to((index_row >> 7).astype(F32), (LANES, LANES)).astype(BF16)
    return hot, high


def pick(hot, high, tile):
    return jnp.where(high == jnp.asarray(tile, BF16), hot, jnp.zeros_like(hot))


def fetch(pairs, sems):
    copies = [pltpu.make_async_copy(a, b, sems.at[k]) for k, (a, b) in enumerate(pairs)]
    for copy in copies:
        copy.start()
    for copy in copies:
        copy.wait()


def gathered(index_ref, proj, hot, out_ref, before_ref=None):
    tiles = proj.shape[0] // LANES
    low, high = column_parts(index_ref[...])
    for block in range(out_ref.shape[0] // EDGE_BLOCK):
        for part in range(EDGE_BLOCK // LANES):
            j = block * (EDGE_BLOCK // LANES) + part
            span = slice(j * LANES, (j + 1) * LANES)
            hot_j, high_j = lane_select(low[:, j : j + 1], high[:, j : j + 1])
            for t in range(tiles):
                hot[span, t * LANES : (t + 1) * LANES] = pick(hot_j, high_j, t)
        span = slice(block * EDGE_BLOCK, (block + 1) * EDGE_BLOCK)
        rows = dot(hot[span], proj[...])
        out_ref[span] = rows if before_ref is None else rows + before_ref[span]


def receiver_kernel(fs_hbm, recv_hbm, w_in_hbm, pre_ref, fs, recv, w_in, proj, hot, sems):
    width = fs.shape[1]
    fetch([(fs_hbm, fs), (recv_hbm, recv), (w_in_hbm.at[pl.ds(width, width)], w_in)], sems)
    proj[...] = dot(fs[...], w_in[...]).astype(BF16)
    gathered(recv, proj, hot, pre_ref)


def sender_kernel(
    before_ref, fs_hbm, send_hbm, w_in_hbm, l3_hbm, recv_ref, pre_ref, l3_rows_ref, inc_ref,
    fs, send, w_in, proj, hot, sems,
):
    width = fs.shape[1]
    wide = lax.axis_index("wide")
    count = lax.axis_size("wide")
    rows = l3_rows_ref.shape[0] // 3
    pairs = [(fs_hbm, fs), (send_hbm, send), (w_in_hbm.at[pl.ds(0, width)], w_in)]
    for k in range(3):
        block = lax.rem(wide + (k + count - 1), count)
        pairs.append(
            (
                l3_hbm.at[pl.ds(pl.multiple_of(block * rows, rows), rows)],
                l3_rows_ref.at[pl.ds(k * rows, rows)],
            )
        )
    fetch(pairs, sems)
    proj[...] = dot(fs[...], w_in[...]).astype(BF16)
    gathered(send, proj, hot, pre_ref, before_ref)
    for j in range(recv_ref.shape[0]):
        hot_r, high_r = row_select(recv_ref[j : j + 1])
        for t in range(inc_ref.shape[0] // LANES):
            inc_ref[t * LANES : (t + 1) * LANES, j * LANES : (j + 1) * LANES] = pick(hot_r, high_r, t)


def fine_kernel(
    pre_ref, around_ref, fs_ref, send_ref, inc_ref, par_ref, w_in_ref, w_out_ref, gain_ref,
    mid_ref, part_ref, hidden, hot,
):
    nodes, width = fs_ref.shape
    edges = pre_ref.shape[0]
    tiles = nodes // LANES
    extra = around_ref.shape[0] // LANES
    proj = dot(around_ref[...], w_in_ref[:width]).astype(BF16)
    send_low, send_high = column_parts(send_ref[...])
    for block in range(edges // EDGE_BLOCK):
        for part in range(EDGE_BLOCK // LANES):
            j = block * (EDGE_BLOCK // LANES) + part
            span = slice(j * LANES, (j + 1) * LANES)
            hot_s, high_s = lane_select(send_low[:, j : j + 1], send_high[:, j : j + 1])
            for t in range(extra):
                hot[span, t * LANES : (t + 1) * LANES] = pick(hot_s, high_s, tiles + t)
        span = slice(block * EDGE_BLOCK, (block + 1) * EDGE_BLOCK)
        hidden[span] = silu(pre_ref[span] + dot(hot[span], proj)).astype(BF16)
    for block in range(nodes // EDGE_BLOCK):
        span = slice(block * EDGE_BLOCK, (block + 1) * EDGE_BLOCK)
        agg = dot(dot(inc_ref[span], hidden[...]).astype(BF16), w_out_ref[...])
        mid_ref[span] = (fs_ref[span].astype(F32) + rms_scale(agg, gain_ref[...])).astype(BF16)
    total = jnp.zeros(part_ref.shape, F32)
    for j in range(tiles):
        hot_p, high_p = row_select(par_ref[j : j + 1])
        upper = jnp.concatenate(
            [pick(hot_p, high_p, t) for t in range(part_ref.shape[0] // LANES)], axis=0
        )
        total = total + dot(upper, mid_ref[j * LANES : (j + 1) * LANES])
    part_ref[...] = total.astype(BF16)


def add_kernel(a_ref, b_ref, out_ref):
    total = (a_ref[...].astype(F32) + b_ref[...].astype(F32)).astype(BF16)
    for k in range(out_ref.shape[0]):
        out_ref[k] = total


def copies_kernel(*refs):
    out_ref = refs[-1]
    for k in range(out_ref.shape[0]):
        start = 0
        for ref in refs[:-1]:
            out_ref[k, start : start + ref.shape[0]] = ref[...]
            start += ref.shape[0]


def coarse_parent(parent_ref, rows, level_three):
    start = (lax.axis_index("wide") - 1) * rows
    local = (parent_ref[...] - start) & (level_three - 1)
    sub = lax.broadcasted_iota(jnp.int32, (3 * rows, LANES), 0)
    return jnp.concatenate(
        [jnp.where(local[j : j + 1] == sub, 1.0, 0.0) for j in range(parent_ref.shape[0])], axis=1
    )


def window_kernel(
    level_three, parts_ref, state_ref, w_up_ref, gain_ref, parent_ref, own_ref, piece_ref, mid_ref
):
    rows = own_ref.shape[0] // 3
    total = parts_ref[0].astype(F32)
    for k in range(1, parts_ref.shape[0]):
        total = total + parts_ref[k].astype(F32)
    level = dot(total.astype(BF16), w_up_ref[...])
    mid = (state_ref[...].astype(F32) + rms_scale(level, gain_ref[...])).astype(BF16)
    mid_ref[...] = mid
    own_ref[...] = dot(coarse_parent(parent_ref, rows, level_three).astype(BF16), mid)
    start = (1 - lax.rem(lax.axis_index("chip"), 2)) * rows
    piece_ref[...] = own_ref[pl.ds(pl.multiple_of(start, rows), 2 * rows)].astype(BF16)


def down_kernel(
    level_three, own_ref, pieces_ref, l3_rows_ref, gain_ref,
    w1_ref, w2_ref, w_down_ref, w_fine_ref, parent_ref, mid_ref, par_ref, fine_ref,
    fine_out_ref, down_ref,
):
    rows = own_ref.shape[0] // 3
    own = own_ref[...]
    behind, ahead, behind2, ahead2 = (pieces_ref[k].astype(F32) for k in range(4))
    total = jnp.concatenate(
        [
            own[:rows] + behind[:rows] + behind2[rows:],
            own[rows : 2 * rows] + behind[rows:] + ahead[:rows],
            own[2 * rows :] + ahead[rows:] + ahead2[:rows],
        ],
        axis=0,
    )
    mid3 = (l3_rows_ref[...].astype(F32) + rms_scale(total, gain_ref[...])).astype(BF16)
    hidden = silu(dot(mid3, w1_ref[...])).astype(BF16)
    new = (mid3.astype(F32) + dot(hidden, w2_ref[...])).astype(BF16)
    lower = coarse_parent(parent_ref, rows, level_three).T.astype(BF16)
    picked = dot(lower, new).astype(BF16)
    down = (mid_ref[...].astype(F32) + dot(picked, w_down_ref[...])).astype(BF16)
    down_ref[...] = down
    fine = dot(down, w_fine_ref[...]).astype(BF16)
    par_low, par_high = column_parts(par_ref[...])
    for j in range(par_ref.shape[0]):
        hot, high = lane_select(par_low[:, j : j + 1], par_high[:, j : j + 1])
        lower = jnp.concatenate([pick(hot, high, t) for t in range(fine.shape[0] // LANES)], axis=1)
        span = slice(j * LANES, (j + 1) * LANES)
        fine_out_ref[span] = (fine_ref[span].astype(F32) + dot(lower, fine)).astype(BF16)


def passed_along(value, steps):
    count = lax.axis_size("wide")
    return lax.ppermute(value, "wide", [(k, (k + steps) % count) for k in range(count)])


def served(value):
    wide, chips, cores = (lax.axis_size(name) for name in ("wide", "chip", "core"))
    steps = (1, -1, 2, -2)
    pairs = []
    for w in range(wide):
        for chip in range(chips):
            for core in range(cores):
                here = chip * cores + core
                pairs.append(
                    (w * chips * cores + here, (w + steps[chip]) % wide * chips * cores + here)
                )
    return lax.ppermute(value, ("wide", "chip", "core"), pairs)


def call(kernel, out, scratch=(), vmem=24, hbm=(), nargs=0, flops=0, moved=0):
    specs = [
        pl.BlockSpec(memory_space=pltpu.HBM if k in hbm else pltpu.VMEM) for k in range(nargs)
    ]
    outs = [jax.ShapeDtypeStruct(shape, dtype) for shape, dtype in out]
    return pl.pallas_call(
        kernel,
        out_shape=outs,
        in_specs=specs,
        out_specs=[pl.BlockSpec(memory_space=pltpu.VMEM) for _ in outs],
        scratch_shapes=list(scratch),
        compiler_params=pltpu.CompilerParams(vmem_limit_bytes=vmem * 2**20),
        cost_estimate=pl.CostEstimate(flops=flops, bytes_accessed=moved, transcendentals=0),
    )


def body(
    fine_state, l2_state, l3_state, boundary, senders, receivers, up_parent, l2_parent, msg_in,
    msg_out, fine_gain, up_weight, l2_gain, l3_gain, l3_w1, l3_w2, down_weight, fine_down,
):
    nodes, width = fine_state.shape
    edges = senders.shape[0]
    level_two = l2_state.shape[0]
    level_three = l3_state.shape[0]
    rows = level_three // lax.axis_size("wide")
    chips, cores = lax.axis_size("chip"), lax.axis_size("core")
    send = senders.reshape(-1, LANES)
    recv = receivers.reshape(-1, LANES)
    par = up_parent.reshape(-1, LANES)
    parent = l2_parent.reshape(-1, LANES)
    fine_gain, l2_gain, l3_gain = (g.reshape(1, width) for g in (fine_gain, l2_gain, l3_gain))

    hot = (boundary[:, None] == jnp.arange(nodes, dtype=jnp.int32)[None, :]).astype(BF16)
    exported = dot(hot, fine_state).astype(BF16)
    behind, ahead = passed_along(exported, 1), passed_along(exported, -1)
    scratch = [
        pltpu.VMEM((nodes, width), BF16),
        pltpu.VMEM(send.shape, jnp.int32),
        pltpu.VMEM((width, width), BF16),
        pltpu.VMEM((nodes, width), BF16),
        pltpu.VMEM((edges, nodes), BF16),
        pltpu.SemaphoreType.DMA((6,)),
    ]
    (pre_recv,) = call(
        receiver_kernel, [((edges, width), F32)], scratch, hbm=(0, 1, 2), nargs=3,
        flops=2_000_000_000, moved=2_000_000,
    )(fine_state, recv, msg_in)
    behind, ahead, pre_recv = lax.optimization_barrier((behind, ahead, pre_recv))
    (window,) = call(
        copies_kernel, [((chips * cores, 3 * boundary.shape[0], width), BF16)], nargs=3
    )(behind, exported, ahead)
    window = lax.all_to_all(window, ("chip", "core"), 0, 0, tiled=True)
    bnd = boundary.shape[0]
    around = window.reshape(chips * cores, 3, bnd, width).transpose(1, 0, 2, 3).reshape(-1, width)

    pre, l3_rows, incidence = call(
        sender_kernel,
        [((edges, width), F32), ((3 * rows, width), BF16), ((nodes, edges), BF16)], scratch,
        hbm=(1, 2, 3, 4), nargs=6, flops=2_000_000_000, moved=2_000_000,
    )(pre_recv, fine_state, send, msg_in, l3_state, recv)

    fine_mid, part = call(
        fine_kernel,
        [((nodes, width), BF16), ((level_two, width), BF16)],
        [pltpu.VMEM((edges, width), BF16), pltpu.VMEM((edges, around.shape[0]), BF16)],
        nargs=9, flops=3_000_000_000, moved=4_000_000,
    )(pre, around, fine_state, send, incidence, par, msg_in, msg_out, fine_gain)

    other = lax.ppermute(part, "core", [(0, 1), (1, 0)])
    (chip_sums,) = call(add_kernel, [((chips, level_two, width), BF16)], nargs=2)(part, other)
    chip_sums = lax.all_to_all(chip_sums, "chip", 0, 0, tiled=True)
    own, piece, l2_mid = call(
        functools.partial(window_kernel, level_three),
        [((3 * rows, width), F32), ((2 * rows, width), BF16), ((level_two, width), BF16)],
        nargs=5,
    )(chip_sums, l2_state, up_weight, l2_gain, parent)
    (pieces,) = call(copies_kernel, [((chips, 2 * rows, width), BF16)], nargs=1)(served(piece))
    pieces = lax.all_to_all(pieces, "chip", 0, 0, tiled=True)

    fine_out, l2_down = call(
        functools.partial(down_kernel, level_three),
        [((nodes, width), BF16), ((level_two, width), BF16)],
        nargs=12,
    )(
        own, pieces, l3_rows, l3_gain, l3_w1, l3_w2, down_weight, fine_down,
        parent, l2_mid, par, fine_mid,
    )
    return (fine_out, l2_down)


def solution(mesh):
    wide, narrow = mesh.devices.shape
    mesh = jax.sharding.Mesh(mesh.devices.reshape(wide, narrow // 2, 2), ("wide", "chip", "core"))
    every = ("wide", "chip", "core")
    return jax.shard_map(
        body,
        mesh=mesh,
        in_specs=(P(every, None), P("wide", None), P()) + (P(every),) * 4 + (P("wide"),) + (P(),) * 10,
        out_specs=(P(every, None), P("wide", None)),
        check_vma=False,
    )
```

```python
import functools

import jax
import jax.numpy as jnp
from jax import lax
from jax.experimental import pallas as pl
from jax.experimental.pallas import tpu as pltpu
from jax.sharding import PartitionSpec as P

F32 = jnp.float32
BF16 = jnp.bfloat16
LANES = 128
EDGE_BLOCK = 512


def dot(a, b):
    return jnp.dot(a, b, preferred_element_type=F32)


def rms_scale(values, gain):
    return values * lax.rsqrt(jnp.mean(values * values, axis=-1, keepdims=True) + 1e-05) * gain


def silu(x):
    half = 0.5 * x
    return half + half * jnp.tanh(half)


def column_parts(index):
    low = (index & (LANES - 1)).astype(F32)
    high = (index >> 7).astype(F32)
    return low.T, high.T


def lane_select(low_col, high_col):
    lane = lax.broadcasted_iota(jnp.int32, (LANES, LANES), 1).astype(F32)
    low = jnp.broadcast_to(low_col, (LANES, LANES))
    hot = jnp.where(low == lane, 1.0, 0.0).astype(BF16)
    high = jnp.broadcast_to(high_col, (LANES, LANES)).astype(BF16)
    return hot, high


def row_select(index_row):
    sub = lax.broadcasted_iota(jnp.int32, (LANES, LANES), 0)
    hot = jnp.where((index_row & (LANES - 1)) == sub, 1.0, 0.0).astype(BF16)
    high = jnp.broadcast_to((index_row >> 7).astype(F32), (LANES, LANES)).astype(BF16)
    return hot, high


def pick(hot, high, tile):
    return jnp.where(high == jnp.asarray(tile, BF16), hot, jnp.zeros_like(hot))


def project_kernel(fs_ref, w_in_ref, send_ref, recv_ref, l3_hbm, proj_ref, cols_ref, l3_rows_ref, sems):
    nodes, width = fs_ref.shape
    wide = lax.axis_index("wide")
    count = lax.axis_size("wide")
    rows = l3_rows_ref.shape[0] // 3
    copies = []
    for k in range(3):
        block = lax.rem(wide + (k + count - 1), count)
        copies.append(
            pltpu.make_async_copy(
                l3_hbm.at[pl.ds(pl.multiple_of(block * rows, rows), rows)],
                l3_rows_ref.at[pl.ds(k * rows, rows)],
                sems.at[k],
            )
        )
    for copy in copies:
        copy.start()
    proj_ref[:nodes] = dot(fs_ref[...], w_in_ref[:width]).astype(BF16)
    proj_ref[nodes:] = dot(fs_ref[...], w_in_ref[width:]).astype(BF16)
    index = jnp.concatenate([send_ref[...], recv_ref[...]], axis=0)
    cols_ref[0], cols_ref[1] = column_parts(index)
    for copy in copies:
        copy.wait()


def gather_kernel(proj_ref, cols_ref, pre_ref, hot):
    edges = pre_ref.shape[0]
    nodes = proj_ref.shape[0] // 2
    groups = edges // LANES
    for block in range(edges // EDGE_BLOCK):
        for part in range(EDGE_BLOCK // LANES):
            j = block * (EDGE_BLOCK // LANES) + part
            span = slice(j * LANES, (j + 1) * LANES)
            for side in range(2):
                k = side * groups + j
                hot_j, high_j = lane_select(cols_ref[0, :, k : k + 1], cols_ref[1, :, k : k + 1])
                for t in range(nodes // LANES):
                    start = side * nodes + t * LANES
                    hot[span, start : start + LANES] = pick(hot_j, high_j, t)
        span = slice(block * EDGE_BLOCK, (block + 1) * EDGE_BLOCK)
        pre_ref[span] = dot(hot[span], proj_ref[...]).astype(BF16)


def fine_kernel(
    pre_ref, around_ref, fs_ref, cols_ref, recv_ref, par_ref, w_in_ref, w_out_ref, gain_ref,
    mid_ref, part_ref, hidden, hot, inc,
):
    nodes, width = fs_ref.shape
    edges = pre_ref.shape[0]
    tiles = nodes // LANES
    extra = around_ref.shape[0] // LANES
    proj = dot(around_ref[...], w_in_ref[:width]).astype(BF16)
    for block in range(edges // EDGE_BLOCK):
        for part in range(EDGE_BLOCK // LANES):
            j = block * (EDGE_BLOCK // LANES) + part
            span = slice(j * LANES, (j + 1) * LANES)
            hot_s, high_s = lane_select(cols_ref[0, :, j : j + 1], cols_ref[1, :, j : j + 1])
            for t in range(extra):
                hot[span, t * LANES : (t + 1) * LANES] = pick(hot_s, high_s, tiles + t)
            hot_r, high_r = row_select(recv_ref[j : j + 1])
            for t in range(tiles):
                inc[t * LANES : (t + 1) * LANES, span] = pick(hot_r, high_r, t)
        span = slice(block * EDGE_BLOCK, (block + 1) * EDGE_BLOCK)
        hidden[span] = silu(pre_ref[span].astype(F32) + dot(hot[span], proj)).astype(BF16)
    for block in range(nodes // EDGE_BLOCK):
        span = slice(block * EDGE_BLOCK, (block + 1) * EDGE_BLOCK)
        agg = dot(dot(inc[span], hidden[...]).astype(BF16), w_out_ref[...])
        mid_ref[span] = (fs_ref[span].astype(F32) + rms_scale(agg, gain_ref[...])).astype(BF16)
    total = jnp.zeros(part_ref.shape, F32)
    for j in range(tiles):
        hot_p, high_p = row_select(par_ref[j : j + 1])
        upper = jnp.concatenate(
            [pick(hot_p, high_p, t) for t in range(part_ref.shape[0] // LANES)], axis=0
        )
        total = total + dot(upper, mid_ref[j * LANES : (j + 1) * LANES])
    part_ref[...] = total.astype(BF16)


def add_kernel(a_ref, b_ref, out_ref):
    total = (a_ref[...].astype(F32) + b_ref[...].astype(F32)).astype(BF16)
    for k in range(out_ref.shape[0]):
        out_ref[k] = total


def copies_kernel(*refs):
    out_ref = refs[-1]
    for k in range(out_ref.shape[0]):
        start = 0
        for ref in refs[:-1]:
            out_ref[k, start : start + ref.shape[0]] = ref[...]
            start += ref.shape[0]


def coarse_parent(parent_ref, rows, level_three):
    start = (lax.axis_index("wide") - 1) * rows
    local = (parent_ref[...] - start) & (level_three - 1)
    sub = lax.broadcasted_iota(jnp.int32, (3 * rows, LANES), 0)
    return jnp.concatenate(
        [jnp.where(local[j : j + 1] == sub, 1.0, 0.0) for j in range(parent_ref.shape[0])], axis=1
    )


def window_kernel(
    level_three, parts_ref, state_ref, w_up_ref, gain_ref, parent_ref, own_ref, piece_ref, mid_ref
):
    rows = own_ref.shape[0] // 3
    total = parts_ref[0].astype(F32)
    for k in range(1, parts_ref.shape[0]):
        total = total + parts_ref[k].astype(F32)
    level = dot(total.astype(BF16), w_up_ref[...])
    mid = (state_ref[...].astype(F32) + rms_scale(level, gain_ref[...])).astype(BF16)
    mid_ref[...] = mid
    own_ref[...] = dot(coarse_parent(parent_ref, rows, level_three).astype(BF16), mid)
    start = (1 - lax.rem(lax.axis_index("chip"), 2)) * rows
    piece_ref[...] = own_ref[pl.ds(pl.multiple_of(start, rows), 2 * rows)].astype(BF16)


def down_kernel(
    level_three, own_ref, pieces_ref, l3_rows_ref, gain_ref,
    w1_ref, w2_ref, w_down_ref, w_fine_ref, parent_ref, mid_ref, par_ref, fine_ref,
    fine_out_ref, down_ref,
):
    rows = own_ref.shape[0] // 3
    own = own_ref[...]
    behind, ahead, behind2, ahead2 = (pieces_ref[k].astype(F32) for k in range(4))
    total = jnp.concatenate(
        [
            own[:rows] + behind[:rows] + behind2[rows:],
            own[rows : 2 * rows] + behind[rows:] + ahead[:rows],
            own[2 * rows :] + ahead[rows:] + ahead2[:rows],
        ],
        axis=0,
    )
    mid3 = (l3_rows_ref[...].astype(F32) + rms_scale(total, gain_ref[...])).astype(BF16)
    hidden = silu(dot(mid3, w1_ref[...])).astype(BF16)
    new = (mid3.astype(F32) + dot(hidden, w2_ref[...])).astype(BF16)
    lower = coarse_parent(parent_ref, rows, level_three).T.astype(BF16)
    picked = dot(lower, new).astype(BF16)
    down = (mid_ref[...].astype(F32) + dot(picked, w_down_ref[...])).astype(BF16)
    down_ref[...] = down
    fine = dot(down, w_fine_ref[...]).astype(BF16)
    par_low, par_high = column_parts(par_ref[...])
    for j in range(par_ref.shape[0]):
        hot, high = lane_select(par_low[:, j : j + 1], par_high[:, j : j + 1])
        lower = jnp.concatenate([pick(hot, high, t) for t in range(fine.shape[0] // LANES)], axis=1)
        span = slice(j * LANES, (j + 1) * LANES)
        fine_out_ref[span] = (fine_ref[span].astype(F32) + dot(lower, fine)).astype(BF16)


def passed_along(value, steps):
    count = lax.axis_size("wide")
    return lax.ppermute(value, "wide", [(k, (k + steps) % count) for k in range(count)])


def served(value):
    wide, chips, cores = (lax.axis_size(name) for name in ("wide", "chip", "core"))
    steps = (1, -1, 2, -2)
    pairs = []
    for w in range(wide):
        for chip in range(chips):
            for core in range(cores):
                here = chip * cores + core
                pairs.append(
                    (w * chips * cores + here, (w + steps[chip]) % wide * chips * cores + here)
                )
    return lax.ppermute(value, ("wide", "chip", "core"), pairs)


def call(kernel, out, scratch=(), vmem=24, hbm=(), nargs=0, flops=0, moved=0):
    specs = [
        pl.BlockSpec(memory_space=pltpu.HBM if k in hbm else pltpu.VMEM) for k in range(nargs)
    ]
    outs = [jax.ShapeDtypeStruct(shape, dtype) for shape, dtype in out]
    return pl.pallas_call(
        kernel,
        out_shape=outs,
        in_specs=specs,
        out_specs=[pl.BlockSpec(memory_space=pltpu.VMEM) for _ in outs],
        scratch_shapes=list(scratch),
        compiler_params=pltpu.CompilerParams(vmem_limit_bytes=vmem * 2**20),
        cost_estimate=pl.CostEstimate(flops=flops, bytes_accessed=moved, transcendentals=0),
    )


def body(
    fine_state, l2_state, l3_state, boundary, senders, receivers, up_parent, l2_parent, msg_in,
    msg_out, fine_gain, up_weight, l2_gain, l3_gain, l3_w1, l3_w2, down_weight, fine_down,
):
    nodes, width = fine_state.shape
    edges = senders.shape[0]
    level_two = l2_state.shape[0]
    level_three = l3_state.shape[0]
    rows = level_three // lax.axis_size("wide")
    chips, cores = lax.axis_size("chip"), lax.axis_size("core")
    send = senders.reshape(-1, LANES)
    recv = receivers.reshape(-1, LANES)
    par = up_parent.reshape(-1, LANES)
    parent = l2_parent.reshape(-1, LANES)
    fine_gain, l2_gain, l3_gain = (g.reshape(1, width) for g in (fine_gain, l2_gain, l3_gain))

    hot = (boundary[:, None] == jnp.arange(nodes, dtype=jnp.int32)[None, :]).astype(BF16)
    exported = dot(hot, fine_state).astype(BF16)
    behind, ahead = passed_along(exported, 1), passed_along(exported, -1)
    proj, cols, l3_rows = call(
        project_kernel,
        [((2 * nodes, width), BF16), ((2, LANES, 2 * send.shape[0]), F32), ((3 * rows, width), BF16)],
        [pltpu.SemaphoreType.DMA((3,))],
        hbm=(4,), nargs=5, vmem=61, flops=500_000_000, moved=2_000_000,
    )(fine_state, msg_in, send, recv, l3_state)
    behind, ahead, proj = lax.optimization_barrier((behind, ahead, proj))
    (window,) = call(
        copies_kernel, [((chips * cores, 3 * boundary.shape[0], width), BF16)], nargs=3
    )(behind, exported, ahead)
    window = lax.all_to_all(window, ("chip", "core"), 0, 0, tiled=True)
    bnd = boundary.shape[0]
    around = window.reshape(chips * cores, 3, bnd, width).transpose(1, 0, 2, 3).reshape(-1, width)

    (pre,) = call(
        gather_kernel, [((edges, width), BF16)], [pltpu.VMEM((edges, 2 * nodes), BF16)],
        nargs=2, flops=4_000_000_000, moved=2_000_000,
    )(proj, cols)

    fine_mid, part = call(
        fine_kernel,
        [((nodes, width), BF16), ((level_two, width), BF16)],
        [
            pltpu.VMEM((edges, width), BF16),
            pltpu.VMEM((edges, around.shape[0]), BF16),
            pltpu.VMEM((nodes, edges), BF16),
        ],
        nargs=9, flops=3_000_000_000, moved=4_000_000,
    )(pre, around, fine_state, cols, recv, par, msg_in, msg_out, fine_gain)

    other = lax.ppermute(part, "core", [(0, 1), (1, 0)])
    (chip_sums,) = call(add_kernel, [((chips, level_two, width), BF16)], nargs=2)(part, other)
    chip_sums = lax.all_to_all(chip_sums, "chip", 0, 0, tiled=True)
    own, piece, l2_mid = call(
        functools.partial(window_kernel, level_three),
        [((3 * rows, width), F32), ((2 * rows, width), BF16), ((level_two, width), BF16)],
        nargs=5,
    )(chip_sums, l2_state, up_weight, l2_gain, parent)
    (pieces,) = call(copies_kernel, [((chips, 2 * rows, width), BF16)], nargs=1)(served(piece))
    pieces = lax.all_to_all(pieces, "chip", 0, 0, tiled=True)

    fine_out, l2_down = call(
        functools.partial(down_kernel, level_three),
        [((nodes, width), BF16), ((level_two, width), BF16)],
        nargs=12,
    )(
        own, pieces, l3_rows, l3_gain, l3_w1, l3_w2, down_weight, fine_down,
        parent, l2_mid, par, fine_mid,
    )
    return (fine_out, l2_down)


def solution(mesh):
    wide, narrow = mesh.devices.shape
    mesh = jax.sharding.Mesh(mesh.devices.reshape(wide, narrow // 2, 2), ("wide", "chip", "core"))
    every = ("wide", "chip", "core")
    return jax.shard_map(
        body,
        mesh=mesh,
        in_specs=(P(every, None), P("wide", None), P()) + (P(every),) * 4 + (P("wide"),) + (P(),) * 10,
        out_specs=(P(every, None), P("wide", None)),
        check_vma=False,
    )
```

```python
import functools

import jax
import jax.numpy as jnp
from jax import lax
from jax.experimental import pallas as pl
from jax.experimental.pallas import tpu as pltpu
from jax.sharding import PartitionSpec as P

F32 = jnp.float32
BF16 = jnp.bfloat16
LANES = 128
EDGE_BLOCK = 512


def dot(a, b):
    return jnp.dot(a, b, preferred_element_type=F32)


def rms_scale(values, gain):
    return values * lax.rsqrt(jnp.mean(values * values, axis=-1, keepdims=True) + 1e-05) * gain


def silu(x):
    half = 0.5 * x
    return half + half * jnp.tanh(half)


def column_parts(index):
    low = (index & (LANES - 1)).astype(F32)
    high = (index >> 7).astype(F32)
    return low.T, high.T


def lane_select(low_col, high_col):
    lane = lax.broadcasted_iota(jnp.int32, (LANES, LANES), 1).astype(F32)
    low = jnp.broadcast_to(low_col, (LANES, LANES))
    hot = jnp.where(low == lane, 1.0, 0.0).astype(BF16)
    high = jnp.broadcast_to(high_col, (LANES, LANES)).astype(BF16)
    return hot, high


def row_select(index_row):
    sub = lax.broadcasted_iota(jnp.int32, (LANES, LANES), 0)
    hot = jnp.where((index_row & (LANES - 1)) == sub, 1.0, 0.0).astype(BF16)
    high = jnp.broadcast_to((index_row >> 7).astype(F32), (LANES, LANES)).astype(BF16)
    return hot, high


def pick(hot, high, tile):
    return jnp.where(high == jnp.asarray(tile, BF16), hot, jnp.zeros_like(hot))


def gather_kernel(fs_ref, w_in_ref, send_ref, recv_ref, l3_hbm, pre_ref, l3_rows_ref, proj, hot, sems):
    nodes, width = fs_ref.shape
    edges = pre_ref.shape[0]
    wide = lax.axis_index("wide")
    count = lax.axis_size("wide")
    rows = l3_rows_ref.shape[0] // 3
    copies = []
    for k in range(3):
        block = lax.rem(wide + (k + count - 1), count)
        copies.append(
            pltpu.make_async_copy(
                l3_hbm.at[pl.ds(pl.multiple_of(block * rows, rows), rows)],
                l3_rows_ref.at[pl.ds(k * rows, rows)],
                sems.at[k],
            )
        )
    for copy in copies:
        copy.start()
    proj[:nodes] = dot(fs_ref[...], w_in_ref[:width]).astype(BF16)
    proj[nodes:] = dot(fs_ref[...], w_in_ref[width:]).astype(BF16)
    columns = [column_parts(send_ref[...]), column_parts(recv_ref[...])]
    for block in range(edges // EDGE_BLOCK):
        for part in range(EDGE_BLOCK // LANES):
            j = block * (EDGE_BLOCK // LANES) + part
            span = slice(j * LANES, (j + 1) * LANES)
            for side, (low, high) in enumerate(columns):
                hot_j, high_j = lane_select(low[:, j : j + 1], high[:, j : j + 1])
                for t in range(nodes // LANES):
                    start = side * nodes + t * LANES
                    hot[span, start : start + LANES] = pick(hot_j, high_j, t)
        span = slice(block * EDGE_BLOCK, (block + 1) * EDGE_BLOCK)
        pre_ref[span] = dot(hot[span], proj[...]).astype(BF16)
    for copy in copies:
        copy.wait()


def chip_rows_kernel(mine_ref, other_ref, out_ref):
    rows = mine_ref.shape[0]
    core = lax.axis_index("core")
    first = jnp.where(core == 0, mine_ref[...], other_ref[...])
    last = jnp.where(core == 0, other_ref[...], mine_ref[...])
    for k in range(out_ref.shape[0]):
        out_ref[k, :rows] = first
        out_ref[k, rows:] = last


def neighbour_kernel(pair_ref, out_ref):
    out_ref[...] = pair_ref[1 - pair_slot()]


def fine_kernel(
    pre_ref, pair_ref, far_ref, fs_ref, send_ref, recv_ref, par_ref, w_in_ref, w_out_ref, gain_ref,
    mid_ref, keep_ref, give_ref, around, hidden, hot, inc, sums,
):
    nodes, width = fs_ref.shape
    edges = pre_ref.shape[0]
    tiles = nodes // LANES
    bound = far_ref.shape[0]
    extra = 3 * bound // LANES
    slot = pair_slot()
    ahead = lax.rem(lax.axis_index("wide") + lax.axis_index("core"), 2) == 0
    near_at, far_at = jnp.where(ahead, 2 * bound, 0), jnp.where(ahead, 0, 2 * bound)
    around[pl.ds(pl.multiple_of(near_at, bound), bound)] = pair_ref[1 - slot]
    around[bound : 2 * bound] = pair_ref[slot]
    around[pl.ds(pl.multiple_of(far_at, bound), bound)] = far_ref[...]
    proj = dot(around[...], w_in_ref[:width]).astype(BF16)
    send_low, send_high = column_parts(send_ref[...])
    for block in range(edges // EDGE_BLOCK):
        for part in range(EDGE_BLOCK // LANES):
            j = block * (EDGE_BLOCK // LANES) + part
            span = slice(j * LANES, (j + 1) * LANES)
            hot_s, high_s = lane_select(send_low[:, j : j + 1], send_high[:, j : j + 1])
            for t in range(extra):
                hot[span, t * LANES : (t + 1) * LANES] = pick(hot_s, high_s, tiles + t)
            hot_r, high_r = row_select(recv_ref[j : j + 1])
            for t in range(tiles):
                inc[t * LANES : (t + 1) * LANES, span] = pick(hot_r, high_r, t)
        span = slice(block * EDGE_BLOCK, (block + 1) * EDGE_BLOCK)
        hidden[span] = silu(pre_ref[span].astype(F32) + dot(hot[span], proj)).astype(BF16)
    for block in range(nodes // EDGE_BLOCK):
        span = slice(block * EDGE_BLOCK, (block + 1) * EDGE_BLOCK)
        agg = dot(dot(inc[span], hidden[...]).astype(BF16), w_out_ref[...])
        mid_ref[span] = (fs_ref[span].astype(F32) + rms_scale(agg, gain_ref[...])).astype(BF16)
    total = jnp.zeros(sums.shape, F32)
    for j in range(tiles):
        hot_p, high_p = row_select(par_ref[j : j + 1])
        upper = jnp.concatenate(
            [pick(hot_p, high_p, t) for t in range(sums.shape[0] // LANES)], axis=0
        )
        total = total + dot(upper, mid_ref[j * LANES : (j + 1) * LANES])
    sums[...] = total
    half = keep_ref.shape[0]
    core = lax.axis_index("core")
    keep_ref[...] = sums[pl.ds(pl.multiple_of(core * half, half), half)].astype(BF16)
    give_ref[...] = sums[pl.ds(pl.multiple_of((1 - core) * half, half), half)].astype(BF16)


def add_kernel(a_ref, b_ref, out_ref):
    total = (a_ref[...].astype(F32) + b_ref[...].astype(F32)).astype(BF16)
    for k in range(out_ref.shape[0]):
        out_ref[k] = total


def level_two_kernel(parts_ref, state_ref, w_up_ref, gain_ref, out_ref):
    rows = out_ref.shape[0]
    total = parts_ref[0].astype(F32)
    for k in range(1, parts_ref.shape[0]):
        total = total + parts_ref[k].astype(F32)
    level = dot(total.astype(BF16), w_up_ref[...])
    start = pl.multiple_of(lax.axis_index("core") * rows, rows)
    state = state_ref[pl.ds(start, rows)].astype(F32)
    out_ref[...] = (state + rms_scale(level, gain_ref[...])).astype(BF16)


def coarse_parent(parent_ref, rows, level_three):
    start = (lax.axis_index("wide") - 1) * rows
    local = (parent_ref[...] - start) & (level_three - 1)
    sub = lax.broadcasted_iota(jnp.int32, (3 * rows, LANES), 0)
    return jnp.concatenate(
        [jnp.where(local[j : j + 1] == sub, 1.0, 0.0) for j in range(parent_ref.shape[0])], axis=1
    )


def window_kernel(level_three, mine_ref, other_ref, parent_ref, own_ref, pieces_ref, mid_ref, padded):
    rows = own_ref.shape[0] // 3
    core = lax.axis_index("core")
    mid = jnp.concatenate(
        [
            jnp.where(core == 0, mine_ref[...], other_ref[...]),
            jnp.where(core == 0, other_ref[...], mine_ref[...]),
        ],
        axis=0,
    )
    mid_ref[...] = mid
    own = dot(coarse_parent(parent_ref, rows, level_three).astype(BF16), mid)
    own_ref[...] = own
    padded[...] = jnp.zeros_like(padded)
    padded[rows : 4 * rows] = own.astype(BF16)
    here = quad_slot()
    for there in range(pieces_ref.shape[0]):
        step = there - here
        start = jnp.where(
            step == 1, 2, jnp.where(step == 2, 3, jnp.where(step == -1, 1, jnp.where(step == -2, 0, 5)))
        )
        start = jnp.where((core == 1) & ((here >= 2) == (there >= 2)), 5, start)
        pieces_ref[there] = padded[pl.ds(pl.multiple_of(start * rows, rows), 2 * rows)]


def collect_kernel(pieces_ref, out_ref, sums):
    rows = out_ref.shape[0] // 3
    sums[...] = jnp.zeros_like(sums)
    here = quad_slot()
    for there in range(pieces_ref.shape[0]):
        start = pl.multiple_of(jnp.where(there < here, 0, rows), rows)
        sums[pl.ds(start, 2 * rows)] += pieces_ref[there].astype(F32)
    out_ref[...] = sums[...].astype(BF16)


def down_kernel(
    level_three, own_ref, mine_ref, other_ref, l3_rows_ref, gain_ref,
    w1_ref, w2_ref, w_down_ref, w_fine_ref, parent_ref, mid_ref, par_ref, fine_ref,
    fine_out_ref, down_ref,
):
    rows = own_ref.shape[0] // 3
    total = own_ref[...] + (mine_ref[...].astype(F32) + other_ref[...].astype(F32))
    mid3 = (l3_rows_ref[...].astype(F32) + rms_scale(total, gain_ref[...])).astype(BF16)
    hidden = silu(dot(mid3, w1_ref[...])).astype(BF16)
    new = (mid3.astype(F32) + dot(hidden, w2_ref[...])).astype(BF16)
    lower = coarse_parent(parent_ref, rows, level_three).T.astype(BF16)
    picked = dot(lower, new).astype(BF16)
    down = (mid_ref[...].astype(F32) + dot(picked, w_down_ref[...])).astype(BF16)
    down_ref[...] = down
    fine = dot(down, w_fine_ref[...]).astype(BF16)
    par_low, par_high = column_parts(par_ref[...])
    for j in range(par_ref.shape[0]):
        hot, high = lane_select(par_low[:, j : j + 1], par_high[:, j : j + 1])
        lower = jnp.concatenate([pick(hot, high, t) for t in range(fine.shape[0] // LANES)], axis=1)
        span = slice(j * LANES, (j + 1) * LANES)
        fine_out_ref[span] = (fine_ref[span].astype(F32) + dot(lower, fine)).astype(BF16)


def pair_slot():
    return lax.rem(lax.axis_index("wide") + lax.axis_index("core"), 2)


def quad_slot():
    return lax.rem(lax.axis_index("wide") + 2 * lax.axis_index("core"), 4)


def device_of(wide, chip, core):
    sizes = [lax.axis_size(name) for name in ("wide", "chip", "core")]
    return (wide % sizes[0] * sizes[1] + chip) * sizes[2] + core


def exchanged(value, groups):
    return lax.all_to_all(
        value, ("wide", "chip", "core"), 0, 0, tiled=True, axis_index_groups=groups
    )


def core_swapped(value):
    return lax.ppermute(value, "core", [(0, 1), (1, 0)])


def call(kernel, out, scratch=(), vmem=24, hbm=(), nargs=0, flops=0, moved=0):
    specs = [
        pl.BlockSpec(memory_space=pltpu.HBM if k in hbm else pltpu.VMEM) for k in range(nargs)
    ]
    outs = [jax.ShapeDtypeStruct(shape, dtype) for shape, dtype in out]
    return pl.pallas_call(
        kernel,
        out_shape=outs,
        in_specs=specs,
        out_specs=[pl.BlockSpec(memory_space=pltpu.VMEM) for _ in outs],
        scratch_shapes=list(scratch),
        compiler_params=pltpu.CompilerParams(vmem_limit_bytes=vmem * 2**20),
        cost_estimate=pl.CostEstimate(flops=flops, bytes_accessed=moved, transcendentals=0),
    )


def body(
    fine_state, l2_state, l3_state, boundary, senders, receivers, up_parent, l2_parent, msg_in,
    msg_out, fine_gain, up_weight, l2_gain, l3_gain, l3_w1, l3_w2, down_weight, fine_down,
):
    nodes, width = fine_state.shape
    edges = senders.shape[0]
    level_two = l2_state.shape[0]
    level_three = l3_state.shape[0]
    wide = lax.axis_size("wide")
    rows = level_three // wide
    chips, cores = lax.axis_size("chip"), lax.axis_size("core")
    send = senders.reshape(-1, LANES)
    recv = receivers.reshape(-1, LANES)
    par = up_parent.reshape(-1, LANES)
    parent = l2_parent.reshape(-1, LANES)
    fine_gain, l2_gain, l3_gain = (g.reshape(1, width) for g in (fine_gain, l2_gain, l3_gain))

    hot = (boundary[:, None] == jnp.arange(nodes, dtype=jnp.int32)[None, :]).astype(BF16)
    exported = dot(hot, fine_state).astype(BF16)
    bound = chips * cores * boundary.shape[0]
    pairs = [
        [device_of(first + core + step, chip, core) for step in range(2) for chip in range(chips)]
        for core in range(cores)
        for first in range(0, wide, 2)
    ]
    quads = [
        [device_of(first + 2 * core + step, chip, core) for step in range(4)]
        for core in range(cores)
        for chip in range(chips)
        for first in range(0, wide, 4)
    ]

    (chip_rows,) = call(
        chip_rows_kernel, [((2 * chips, cores * boundary.shape[0], width), BF16)], nargs=2
    )(exported, core_swapped(exported))
    chip_rows, local_state = lax.optimization_barrier((chip_rows, fine_state))
    pair = exchanged(chip_rows, pairs).reshape(2, bound, width)

    pre, l3_rows = call(
        gather_kernel,
        [((edges, width), BF16), ((3 * rows, width), BF16)],
        [
            pltpu.VMEM((2 * nodes, width), BF16),
            pltpu.VMEM((edges, 2 * nodes), BF16),
            pltpu.SemaphoreType.DMA((3,)),
        ],
        hbm=(4,), nargs=5, vmem=61, flops=5_000_000_000, moved=2_000_000,
    )(local_state, msg_in, send, recv, l3_state)
    pair, pre = lax.optimization_barrier((pair, pre))
    (near,) = call(neighbour_kernel, [((bound, width), BF16)], nargs=1)(pair)
    far = core_swapped(near)

    half = level_two // 2
    fine_mid, keep, give = call(
        fine_kernel,
        [((nodes, width), BF16), ((half, width), BF16), ((half, width), BF16)],
        [
            pltpu.VMEM((3 * bound, width), BF16),
            pltpu.VMEM((edges, width), BF16),
            pltpu.VMEM((edges, 3 * bound), BF16),
            pltpu.VMEM((nodes, edges), BF16),
            pltpu.VMEM((level_two, width), F32),
        ],
        nargs=10, flops=3_000_000_000, moved=4_000_000,
    )(pre, pair, far, fine_state, send, recv, par, msg_in, msg_out, fine_gain)

    (chip_sums,) = call(add_kernel, [((chips, half, width), BF16)], nargs=2)(keep, core_swapped(give))
    chip_sums = lax.all_to_all(chip_sums, "chip", 0, 0, tiled=True)
    (half_mid,) = call(level_two_kernel, [((half, width), BF16)], nargs=4)(
        chip_sums, l2_state, up_weight, l2_gain
    )
    own, pieces, l2_mid = call(
        functools.partial(window_kernel, level_three),
        [((3 * rows, width), F32), ((4, 2 * rows, width), BF16), ((level_two, width), BF16)],
        [pltpu.VMEM((7 * rows, width), BF16)],
        nargs=3,
    )(half_mid, core_swapped(half_mid), parent)
    (mine,) = call(
        collect_kernel, [((3 * rows, width), BF16)], [pltpu.VMEM((3 * rows, width), F32)], nargs=1
    )(exchanged(pieces, quads))

    fine_out, l2_down = call(
        functools.partial(down_kernel, level_three),
        [((nodes, width), BF16), ((level_two, width), BF16)],
        nargs=13,
    )(
        own, mine, core_swapped(mine), l3_rows, l3_gain, l3_w1, l3_w2, down_weight, fine_down,
        parent, l2_mid, par, fine_mid,
    )
    return (fine_out, l2_down)


def solution(mesh):
    wide, narrow = mesh.devices.shape
    mesh = jax.sharding.Mesh(mesh.devices.reshape(wide, narrow // 2, 2), ("wide", "chip", "core"))
    every = ("wide", "chip", "core")
    return jax.shard_map(
        body,
        mesh=mesh,
        in_specs=(P(every, None), P("wide", None), P()) + (P(every),) * 4 + (P("wide"),) + (P(),) * 10,
        out_specs=(P(every, None), P("wide", None)),
        check_vma=False,
    )
```

```python
import functools

import jax
import jax.numpy as jnp
from jax import lax
from jax.experimental import pallas as pl
from jax.experimental.pallas import tpu as pltpu
from jax.sharding import PartitionSpec as P

F32 = jnp.float32
BF16 = jnp.bfloat16
LANES = 128
EDGE_BLOCK = 512


def dot(a, b):
    return jnp.dot(a, b, preferred_element_type=F32)


def rms_scale(values, gain):
    return values * lax.rsqrt(jnp.mean(values * values, axis=-1, keepdims=True) + 1e-05) * gain


def silu(x):
    half = 0.5 * x
    return half + half * jnp.tanh(half)


def column_parts(index):
    low = (index & (LANES - 1)).astype(F32)
    high = (index >> 7).astype(F32)
    return low.T, high.T


def lane_select(low_col, high_col):
    lane = lax.broadcasted_iota(jnp.int32, (LANES, LANES), 1).astype(F32)
    low = jnp.broadcast_to(low_col, (LANES, LANES))
    hot = jnp.where(low == lane, 1.0, 0.0).astype(BF16)
    high = jnp.broadcast_to(high_col, (LANES, LANES)).astype(BF16)
    return hot, high


def row_select(index_row):
    sub = lax.broadcasted_iota(jnp.int32, (LANES, LANES), 0)
    hot = jnp.where((index_row & (LANES - 1)) == sub, 1.0, 0.0).astype(BF16)
    high = jnp.broadcast_to((index_row >> 7).astype(F32), (LANES, LANES)).astype(BF16)
    return hot, high


def pick(hot, high, tile):
    return jnp.where(high == jnp.asarray(tile, BF16), hot, jnp.zeros_like(hot))


def gather_kernel(
    fs_hbm, w_in_hbm, send_hbm, recv_hbm, l3_hbm, pre_hbm, l3_rows_hbm,
    fs, w_in, send, recv, proj, hot, pre, sems,
):
    nodes, width = fs.shape
    edges = pre.shape[0]
    wide = lax.axis_index("wide")
    count = lax.axis_size("wide")
    rows = l3_rows_hbm.shape[0] // 3
    pairs = [(send_hbm, send), (recv_hbm, recv), (w_in_hbm, w_in), (fs_hbm, fs)]
    for k in range(3):
        block = lax.rem(wide + (k + count - 1), count)
        source = l3_hbm.at[pl.ds(pl.multiple_of(block * rows, rows), rows)]
        pairs.append((source, l3_rows_hbm.at[pl.ds(k * rows, rows)]))
    blocks = edges // EDGE_BLOCK
    for block in range(blocks):
        span = pl.ds(block * EDGE_BLOCK, EDGE_BLOCK)
        pairs.append((pre.at[span], pre_hbm.at[span]))
    copies = [pltpu.make_async_copy(a, b, sems.at[k]) for k, (a, b) in enumerate(pairs)]
    for copy in copies[:7]:
        copy.start()
    copies[0].wait()
    copies[1].wait()
    columns = [column_parts(send[...]), column_parts(recv[...])]
    for block in range(blocks):
        for part in range(EDGE_BLOCK // LANES):
            j = block * (EDGE_BLOCK // LANES) + part
            span = slice(j * LANES, (j + 1) * LANES)
            for side, (low, high) in enumerate(columns):
                hot_j, high_j = lane_select(low[:, j : j + 1], high[:, j : j + 1])
                for t in range(nodes // LANES):
                    start = side * nodes + t * LANES
                    hot[span, start : start + LANES] = pick(hot_j, high_j, t)
        if block == 0:
            copies[2].wait()
            copies[3].wait()
            proj[:nodes] = dot(fs[...], w_in[:width]).astype(BF16)
            proj[nodes:] = dot(fs[...], w_in[width:]).astype(BF16)
        span = slice(block * EDGE_BLOCK, (block + 1) * EDGE_BLOCK)
        pre[span] = dot(hot[span], proj[...]).astype(BF16)
        copies[7 + block].start()
    for copy in copies[4:]:
        copy.wait()


def chip_rows_kernel(mine_ref, other_ref, out_ref):
    rows = mine_ref.shape[0]
    core = lax.axis_index("core")
    first = jnp.where(core == 0, mine_ref[...], other_ref[...])
    last = jnp.where(core == 0, other_ref[...], mine_ref[...])
    for k in range(out_ref.shape[0]):
        out_ref[k, :rows] = first
        out_ref[k, rows:] = last


def neighbour_kernel(pair_ref, out_ref):
    out_ref[...] = pair_ref[1 - pair_slot()]


def prepare_kernel(send_ref, recv_ref, hot_ref, inc_ref):
    tiles = inc_ref.shape[0] // LANES
    low, high = column_parts(send_ref[...])
    for j in range(send_ref.shape[0]):
        span = slice(j * LANES, (j + 1) * LANES)
        hot_s, high_s = lane_select(low[:, j : j + 1], high[:, j : j + 1])
        for t in range(hot_ref.shape[1] // LANES):
            hot_ref[span, t * LANES : (t + 1) * LANES] = pick(hot_s, high_s, tiles + t)
        hot_r, high_r = row_select(recv_ref[j : j + 1])
        for t in range(tiles):
            inc_ref[t * LANES : (t + 1) * LANES, span] = pick(hot_r, high_r, t)


def fine_kernel(
    pre_ref, pair_ref, far_ref, fs_ref, hot_ref, inc_ref, par_ref, w_in_ref, w_out_ref, gain_ref,
    mid_ref, part_ref, around, hidden,
):
    nodes, width = fs_ref.shape
    edges = pre_ref.shape[0]
    tiles = nodes // LANES
    bound = far_ref.shape[0]
    slot = pair_slot()
    ahead = lax.rem(lax.axis_index("wide") + lax.axis_index("core"), 2) == 0
    near_at, far_at = jnp.where(ahead, 2 * bound, 0), jnp.where(ahead, 0, 2 * bound)
    around[pl.ds(pl.multiple_of(near_at, bound), bound)] = pair_ref[1 - slot]
    around[bound : 2 * bound] = pair_ref[slot]
    around[pl.ds(pl.multiple_of(far_at, bound), bound)] = far_ref[...]
    proj = dot(around[...], w_in_ref[:width]).astype(BF16)
    for block in range(edges // EDGE_BLOCK):
        span = slice(block * EDGE_BLOCK, (block + 1) * EDGE_BLOCK)
        hidden[span] = silu(pre_ref[span].astype(F32) + dot(hot_ref[span], proj)).astype(BF16)
    for block in range(nodes // EDGE_BLOCK):
        span = slice(block * EDGE_BLOCK, (block + 1) * EDGE_BLOCK)
        agg = dot(dot(inc_ref[span], hidden[...]).astype(BF16), w_out_ref[...])
        mid_ref[span] = (fs_ref[span].astype(F32) + rms_scale(agg, gain_ref[...])).astype(BF16)
    cores, half, _ = part_ref.shape
    total = jnp.zeros((cores * half, width), F32)
    for j in range(tiles):
        hot_p, high_p = row_select(par_ref[j : j + 1])
        upper = jnp.concatenate([pick(hot_p, high_p, t) for t in range(cores * half // LANES)], axis=0)
        total = total + dot(upper, mid_ref[j * LANES : (j + 1) * LANES])
    for core in range(cores):
        part_ref[core] = total[core * half : (core + 1) * half].astype(BF16)


def add_kernel(parts_ref, out_ref):
    total = (parts_ref[0].astype(F32) + parts_ref[1].astype(F32)).astype(BF16)
    for k in range(out_ref.shape[0]):
        out_ref[k] = total


def level_two_kernel(parts_ref, state_ref, w_up_ref, gain_ref, out_ref):
    rows = out_ref.shape[1]
    total = parts_ref[0].astype(F32)
    for k in range(1, parts_ref.shape[0]):
        total = total + parts_ref[k].astype(F32)
    level = dot(total.astype(BF16), w_up_ref[...])
    start = pl.multiple_of(lax.axis_index("core") * rows, rows)
    state = state_ref[pl.ds(start, rows)].astype(F32)
    mid = (state + rms_scale(level, gain_ref[...])).astype(BF16)
    for k in range(out_ref.shape[0]):
        out_ref[k] = mid


def coarse_parent(parent_ref, rows, level_three):
    start = (lax.axis_index("wide") - 1) * rows
    local = (parent_ref[...] - start) & (level_three - 1)
    sub = lax.broadcasted_iota(jnp.int32, (3 * rows, LANES), 0)
    return jnp.concatenate(
        [jnp.where(local[j : j + 1] == sub, 1.0, 0.0) for j in range(parent_ref.shape[0])], axis=1
    )


def window_kernel(level_three, mid_ref, parent_ref, own_ref, pieces_ref, padded):
    rows = own_ref.shape[0] // 3
    core = lax.axis_index("core")
    own = dot(coarse_parent(parent_ref, rows, level_three).astype(BF16), mid_ref[...])
    own_ref[...] = own
    padded[...] = jnp.zeros_like(padded)
    padded[rows : 4 * rows] = own.astype(BF16)
    here = quad_slot()
    for there in range(pieces_ref.shape[0]):
        step = there - here
        start = jnp.where(
            step == 1, 2, jnp.where(step == 2, 3, jnp.where(step == -1, 1, jnp.where(step == -2, 0, 5)))
        )
        start = jnp.where((core == 1) & ((here >= 2) == (there >= 2)), 5, start)
        pieces_ref[there] = padded[pl.ds(pl.multiple_of(start * rows, rows), 2 * rows)]


def collect_kernel(pieces_ref, out_ref, sums):
    rows = out_ref.shape[1] // 3
    sums[...] = jnp.zeros_like(sums)
    here = quad_slot()
    for there in range(pieces_ref.shape[0]):
        start = pl.multiple_of(jnp.where(there < here, 0, rows), rows)
        sums[pl.ds(start, 2 * rows)] += pieces_ref[there].astype(F32)
    for k in range(out_ref.shape[0]):
        out_ref[k] = sums[...].astype(BF16)


def down_kernel(
    level_three, own_ref, sums_ref, l3_rows_ref, gain_ref,
    w1_ref, w2_ref, w_down_ref, w_fine_ref, parent_ref, mid_ref, par_ref, fine_ref,
    fine_out_ref, down_ref,
):
    rows = own_ref.shape[0] // 3
    total = own_ref[...] + (sums_ref[0].astype(F32) + sums_ref[1].astype(F32))
    mid3 = (l3_rows_ref[...].astype(F32) + rms_scale(total, gain_ref[...])).astype(BF16)
    hidden = silu(dot(mid3, w1_ref[...])).astype(BF16)
    new = (mid3.astype(F32) + dot(hidden, w2_ref[...])).astype(BF16)
    lower = coarse_parent(parent_ref, rows, level_three).T.astype(BF16)
    picked = dot(lower, new).astype(BF16)
    down = (mid_ref[...].astype(F32) + dot(picked, w_down_ref[...])).astype(BF16)
    down_ref[...] = down
    fine = dot(down, w_fine_ref[...]).astype(BF16)
    par_low, par_high = column_parts(par_ref[...])
    for j in range(par_ref.shape[0]):
        hot, high = lane_select(par_low[:, j : j + 1], par_high[:, j : j + 1])
        lower = jnp.concatenate([pick(hot, high, t) for t in range(fine.shape[0] // LANES)], axis=1)
        span = slice(j * LANES, (j + 1) * LANES)
        fine_out_ref[span] = (fine_ref[span].astype(F32) + dot(lower, fine)).astype(BF16)


def pair_slot():
    return lax.rem(lax.axis_index("wide") + lax.axis_index("core"), 2)


def quad_slot():
    return lax.rem(lax.axis_index("wide") + 2 * lax.axis_index("core"), 4)


def device_of(wide, chip, core):
    sizes = [lax.axis_size(name) for name in ("wide", "chip", "core")]
    return (wide % sizes[0] * sizes[1] + chip) * sizes[2] + core


def exchanged(value, groups):
    return lax.all_to_all(
        value, ("wide", "chip", "core"), 0, 0, tiled=True, axis_index_groups=groups
    )


def between_cores(value):
    return lax.all_to_all(value, "core", 0, 0, tiled=True)


def core_swapped(value):
    return lax.ppermute(value, "core", [(0, 1), (1, 0)])


def call(kernel, out, scratch=(), vmem=24, hbm=(), hbm_outs=False, nargs=0, flops=0, moved=0):
    specs = [
        pl.BlockSpec(memory_space=pl.ANY if k in hbm else pltpu.VMEM) for k in range(nargs)
    ]
    outs = [jax.ShapeDtypeStruct(shape, dtype) for shape, dtype in out]
    return pl.pallas_call(
        kernel,
        out_shape=outs,
        in_specs=specs,
        out_specs=[pl.BlockSpec(memory_space=pl.ANY if hbm_outs else pltpu.VMEM) for _ in outs],
        scratch_shapes=list(scratch),
        compiler_params=pltpu.CompilerParams(vmem_limit_bytes=vmem * 2**20),
        cost_estimate=pl.CostEstimate(flops=flops, bytes_accessed=moved, transcendentals=0),
    )


def body(
    fine_state, l2_state, l3_state, boundary, senders, receivers, up_parent, l2_parent, msg_in,
    msg_out, fine_gain, up_weight, l2_gain, l3_gain, l3_w1, l3_w2, down_weight, fine_down,
):
    nodes, width = fine_state.shape
    edges = senders.shape[0]
    level_two = l2_state.shape[0]
    level_three = l3_state.shape[0]
    wide = lax.axis_size("wide")
    rows = level_three // wide
    chips, cores = lax.axis_size("chip"), lax.axis_size("core")
    send = senders.reshape(-1, LANES)
    recv = receivers.reshape(-1, LANES)
    par = up_parent.reshape(-1, LANES)
    parent = l2_parent.reshape(-1, LANES)
    fine_gain, l2_gain, l3_gain = (g.reshape(1, width) for g in (fine_gain, l2_gain, l3_gain))

    hot = (boundary[:, None] == jnp.arange(nodes, dtype=jnp.int32)[None, :]).astype(BF16)
    exported = dot(hot, fine_state).astype(BF16)
    bound = chips * cores * boundary.shape[0]
    pairs = [
        [device_of(first + core + step, chip, core) for step in range(2) for chip in range(chips)]
        for core in range(cores)
        for first in range(0, wide, 2)
    ]
    quads = [
        [device_of(first + 2 * core + step, chip, core) for step in range(4)]
        for core in range(cores)
        for chip in range(chips)
        for first in range(0, wide, 4)
    ]

    (chip_rows,) = call(
        chip_rows_kernel, [((2 * chips, cores * boundary.shape[0], width), BF16)], nargs=2
    )(exported, core_swapped(exported))
    chip_rows, local_state = lax.optimization_barrier((chip_rows, fine_state))
    pair = exchanged(chip_rows, pairs).reshape(2, bound, width)

    pre, l3_rows = call(
        gather_kernel,
        [((edges, width), BF16), ((3 * rows, width), BF16)],
        [
            pltpu.VMEM((nodes, width), BF16),
            pltpu.VMEM((2 * width, width), BF16),
            pltpu.VMEM(send.shape, jnp.int32),
            pltpu.VMEM(recv.shape, jnp.int32),
            pltpu.VMEM((2 * nodes, width), BF16),
            pltpu.VMEM((edges, 2 * nodes), BF16),
            pltpu.VMEM((edges, width), BF16),
            pltpu.SemaphoreType.DMA((7 + edges // EDGE_BLOCK,)),
        ],
        hbm=range(5), hbm_outs=True, nargs=5, vmem=60, flops=5_000_000_000, moved=2_000_000,
    )(local_state, msg_in, send, recv, l3_state)
    pair, pre = lax.optimization_barrier((pair, pre))
    (near,) = call(neighbour_kernel, [((bound, width), BF16)], nargs=1)(pair)
    far = core_swapped(near)
    near, send_late = lax.optimization_barrier((near, send))
    hot, incidence = call(
        prepare_kernel, [((edges, 3 * bound), BF16), ((nodes, edges), BF16)],
        nargs=2, flops=1_000_000_000, moved=6_000_000,
    )(send_late, recv)
    far, hot, incidence = lax.optimization_barrier((far, hot, incidence))

    half = level_two // cores
    fine_mid, part = call(
        fine_kernel,
        [((nodes, width), BF16), ((cores, half, width), BF16)],
        [pltpu.VMEM((3 * bound, width), BF16), pltpu.VMEM((edges, width), BF16)],
        nargs=10, flops=3_000_000_000, moved=4_000_000,
    )(pre, pair, far, fine_state, hot, incidence, par, msg_in, msg_out, fine_gain)

    (chip_sums,) = call(add_kernel, [((chips, half, width), BF16)], nargs=1)(between_cores(part))
    chip_sums = lax.all_to_all(chip_sums, "chip", 0, 0, tiled=True)
    (half_mid,) = call(level_two_kernel, [((cores, half, width), BF16)], nargs=4)(
        chip_sums, l2_state, up_weight, l2_gain
    )
    l2_mid = between_cores(half_mid).reshape(level_two, width)
    own, pieces = call(
        functools.partial(window_kernel, level_three),
        [((3 * rows, width), F32), ((4, 2 * rows, width), BF16)],
        [pltpu.VMEM((7 * rows, width), BF16)],
        nargs=2,
    )(l2_mid, parent)
    (sums,) = call(
        collect_kernel, [((cores, 3 * rows, width), BF16)], [pltpu.VMEM((3 * rows, width), F32)],
        nargs=1,
    )(exchanged(pieces, quads))

    fine_out, l2_down = call(
        functools.partial(down_kernel, level_three),
        [((nodes, width), BF16), ((level_two, width), BF16)],
        nargs=12,
    )(
        own, between_cores(sums), l3_rows, l3_gain, l3_w1, l3_w2, down_weight, fine_down,
        parent, l2_mid, par, fine_mid,
    )
    return (fine_out, l2_down)


def solution(mesh):
    wide, narrow = mesh.devices.shape
    mesh = jax.sharding.Mesh(mesh.devices.reshape(wide, narrow // 2, 2), ("wide", "chip", "core"))
    every = ("wide", "chip", "core")
    return jax.shard_map(
        body,
        mesh=mesh,
        in_specs=(P(every, None), P("wide", None), P()) + (P(every),) * 4 + (P("wide"),) + (P(),) * 10,
        out_specs=(P(every, None), P("wide", None)),
        check_vma=False,
    )
```

```python
import functools

import jax
import jax.numpy as jnp
from jax import lax
from jax.experimental import pallas as pl
from jax.experimental.pallas import tpu as pltpu
from jax.sharding import PartitionSpec as P

F32 = jnp.float32
BF16 = jnp.bfloat16
LANES = 128
EDGE_BLOCK = 512


def dot(a, b):
    return jnp.dot(a, b, preferred_element_type=F32)


def rms_scale(values, gain):
    return values * lax.rsqrt(jnp.mean(values * values, axis=-1, keepdims=True) + 1e-05) * gain


def silu(x):
    half = 0.5 * x
    return half + half * jnp.tanh(half)


def column_parts(index):
    low = (index & (LANES - 1)).astype(F32)
    high = (index >> 7).astype(F32)
    return low.T, high.T


def lane_select(low_col, high_col):
    lane = lax.broadcasted_iota(jnp.int32, (LANES, LANES), 1).astype(F32)
    low = jnp.broadcast_to(low_col, (LANES, LANES))
    hot = jnp.where(low == lane, 1.0, 0.0).astype(BF16)
    high = jnp.broadcast_to(high_col, (LANES, LANES)).astype(BF16)
    return hot, high


def row_select(index_row):
    sub = lax.broadcasted_iota(jnp.int32, (LANES, LANES), 0)
    hot = jnp.where((index_row & (LANES - 1)) == sub, 1.0, 0.0).astype(BF16)
    high = jnp.broadcast_to((index_row >> 7).astype(F32), (LANES, LANES)).astype(BF16)
    return hot, high


def pick(hot, high, tile):
    return jnp.where(high == jnp.asarray(tile, BF16), hot, jnp.zeros_like(hot))


def gather_kernel(
    fs_hbm, w_in_hbm, send_hbm, recv_hbm, l3_hbm, pre_hbm, l3_rows_hbm,
    fs, w_in, send, recv, proj, hot, pre, sems,
):
    nodes, width = fs.shape
    edges = pre.shape[0]
    wide = lax.axis_index("wide")
    count = lax.axis_size("wide")
    rows = l3_rows_hbm.shape[0] // 3
    pairs = [(send_hbm, send), (recv_hbm, recv), (w_in_hbm, w_in), (fs_hbm, fs)]
    for k in range(3):
        block = lax.rem(wide + (k + count - 1), count)
        source = l3_hbm.at[pl.ds(pl.multiple_of(block * rows, rows), rows)]
        pairs.append((source, l3_rows_hbm.at[pl.ds(k * rows, rows)]))
    blocks = edges // EDGE_BLOCK
    for block in range(blocks):
        span = pl.ds(block * EDGE_BLOCK, EDGE_BLOCK)
        pairs.append((pre.at[span], pre_hbm.at[span]))
    copies = [pltpu.make_async_copy(a, b, sems.at[k]) for k, (a, b) in enumerate(pairs)]
    for copy in copies[:7]:
        copy.start()
    copies[0].wait()
    copies[1].wait()
    columns = [column_parts(send[...]), column_parts(recv[...])]
    for block in range(blocks):
        for part in range(EDGE_BLOCK // LANES):
            j = block * (EDGE_BLOCK // LANES) + part
            span = slice(j * LANES, (j + 1) * LANES)
            for side, (low, high) in enumerate(columns):
                hot_j, high_j = lane_select(low[:, j : j + 1], high[:, j : j + 1])
                for t in range(nodes // LANES):
                    start = side * nodes + t * LANES
                    hot[span, start : start + LANES] = pick(hot_j, high_j, t)
        if block == 0:
            copies[2].wait()
            copies[3].wait()
            proj[:nodes] = dot(fs[...], w_in[:width]).astype(BF16)
            proj[nodes:] = dot(fs[...], w_in[width:]).astype(BF16)
        span = slice(block * EDGE_BLOCK, (block + 1) * EDGE_BLOCK)
        pre[span] = dot(hot[span], proj[...]).astype(BF16)
        copies[7 + block].start()
    for copy in copies[4:]:
        copy.wait()


def chip_rows_kernel(mine_ref, other_ref, out_ref):
    rows = mine_ref.shape[0]
    core = lax.axis_index("core")
    first = jnp.where(core == 0, mine_ref[...], other_ref[...])
    last = jnp.where(core == 0, other_ref[...], mine_ref[...])
    for k in range(out_ref.shape[0]):
        out_ref[k, :rows] = first
        out_ref[k, rows:] = last


def neighbour_kernel(pair_ref, out_ref):
    out_ref[...] = pair_ref[1 - pair_slot()]


def prepare_kernel(send_ref, recv_ref, hot_ref, inc_ref):
    tiles = inc_ref.shape[0] // LANES
    low, high = column_parts(send_ref[...])
    for j in range(send_ref.shape[0]):
        span = slice(j * LANES, (j + 1) * LANES)
        hot_s, high_s = lane_select(low[:, j : j + 1], high[:, j : j + 1])
        for t in range(hot_ref.shape[1] // LANES):
            hot_ref[span, t * LANES : (t + 1) * LANES] = pick(hot_s, high_s, tiles + t)
        hot_r, high_r = row_select(recv_ref[j : j + 1])
        for t in range(tiles):
            inc_ref[t * LANES : (t + 1) * LANES, span] = pick(hot_r, high_r, t)


def fine_kernel(
    pre_ref, pair_ref, far_ref, fs_ref, hot_ref, inc_ref, par_ref, w_in_ref, w_out_ref, gain_ref,
    mid_ref, keep_ref, give_ref, around, hidden, sums,
):
    nodes, width = fs_ref.shape
    edges = pre_ref.shape[0]
    tiles = nodes // LANES
    bound = far_ref.shape[0]
    slot = pair_slot()
    ahead = lax.rem(lax.axis_index("wide") + lax.axis_index("core"), 2) == 0
    near_at, far_at = jnp.where(ahead, 2 * bound, 0), jnp.where(ahead, 0, 2 * bound)
    around[pl.ds(pl.multiple_of(near_at, bound), bound)] = pair_ref[1 - slot]
    around[bound : 2 * bound] = pair_ref[slot]
    around[pl.ds(pl.multiple_of(far_at, bound), bound)] = far_ref[...]
    proj = dot(around[...], w_in_ref[:width]).astype(BF16)
    for block in range(edges // EDGE_BLOCK):
        span = slice(block * EDGE_BLOCK, (block + 1) * EDGE_BLOCK)
        hidden[span] = silu(pre_ref[span].astype(F32) + dot(hot_ref[span], proj)).astype(BF16)
    for block in range(nodes // EDGE_BLOCK):
        span = slice(block * EDGE_BLOCK, (block + 1) * EDGE_BLOCK)
        agg = dot(dot(inc_ref[span], hidden[...]).astype(BF16), w_out_ref[...])
        mid_ref[span] = (fs_ref[span].astype(F32) + rms_scale(agg, gain_ref[...])).astype(BF16)
    total = jnp.zeros(sums.shape, F32)
    for j in range(tiles):
        hot_p, high_p = row_select(par_ref[j : j + 1])
        upper = jnp.concatenate(
            [pick(hot_p, high_p, t) for t in range(sums.shape[0] // LANES)], axis=0
        )
        total = total + dot(upper, mid_ref[j * LANES : (j + 1) * LANES])
    sums[...] = total
    half = keep_ref.shape[0]
    core = lax.axis_index("core")
    keep_ref[...] = sums[pl.ds(pl.multiple_of(core * half, half), half)].astype(BF16)
    give_ref[...] = sums[pl.ds(pl.multiple_of((1 - core) * half, half), half)].astype(BF16)


def add_kernel(a_ref, b_ref, out_ref):
    total = (a_ref[...].astype(F32) + b_ref[...].astype(F32)).astype(BF16)
    for k in range(out_ref.shape[0]):
        out_ref[k] = total


def level_two_kernel(parts_ref, state_ref, w_up_ref, gain_ref, out_ref):
    rows = out_ref.shape[0]
    total = parts_ref[0].astype(F32)
    for k in range(1, parts_ref.shape[0]):
        total = total + parts_ref[k].astype(F32)
    level = dot(total.astype(BF16), w_up_ref[...])
    start = pl.multiple_of(lax.axis_index("core") * rows, rows)
    state = state_ref[pl.ds(start, rows)].astype(F32)
    out_ref[...] = (state + rms_scale(level, gain_ref[...])).astype(BF16)


def coarse_parent(parent_ref, rows, level_three):
    start = (lax.axis_index("wide") - 1) * rows
    local = (parent_ref[...] - start) & (level_three - 1)
    sub = lax.broadcasted_iota(jnp.int32, (3 * rows, LANES), 0)
    return jnp.concatenate(
        [jnp.where(local[j : j + 1] == sub, 1.0, 0.0) for j in range(parent_ref.shape[0])], axis=1
    )


def window_kernel(level_three, mine_ref, other_ref, parent_ref, own_ref, pieces_ref, mid_ref, padded):
    rows = own_ref.shape[0] // 3
    core = lax.axis_index("core")
    mid = jnp.concatenate(
        [
            jnp.where(core == 0, mine_ref[...], other_ref[...]),
            jnp.where(core == 0, other_ref[...], mine_ref[...]),
        ],
        axis=0,
    )
    mid_ref[...] = mid
    own = dot(coarse_parent(parent_ref, rows, level_three).astype(BF16), mid)
    own_ref[...] = own
    padded[...] = jnp.zeros_like(padded)
    padded[rows : 4 * rows] = own.astype(BF16)
    here = quad_slot()
    for there in range(pieces_ref.shape[0]):
        step = there - here
        start = jnp.where(
            step == 1, 2, jnp.where(step == 2, 3, jnp.where(step == -1, 1, jnp.where(step == -2, 0, 5)))
        )
        start = jnp.where((core == 1) & ((here >= 2) == (there >= 2)), 5, start)
        pieces_ref[there] = padded[pl.ds(pl.multiple_of(start * rows, rows), 2 * rows)]


def collect_kernel(pieces_ref, out_ref, sums):
    rows = out_ref.shape[0] // 3
    sums[...] = jnp.zeros_like(sums)
    here = quad_slot()
    for there in range(pieces_ref.shape[0]):
        start = pl.multiple_of(jnp.where(there < here, 0, rows), rows)
        sums[pl.ds(start, 2 * rows)] += pieces_ref[there].astype(F32)
    out_ref[...] = sums[...].astype(BF16)


def down_kernel(
    level_three, own_ref, mine_ref, other_ref, l3_rows_ref, gain_ref,
    w1_ref, w2_ref, w_down_ref, w_fine_ref, parent_ref, mid_ref, par_ref, fine_ref,
    fine_out_ref, down_ref,
):
    rows = own_ref.shape[0] // 3
    total = own_ref[...] + (mine_ref[...].astype(F32) + other_ref[...].astype(F32))
    mid3 = (l3_rows_ref[...].astype(F32) + rms_scale(total, gain_ref[...])).astype(BF16)
    hidden = silu(dot(mid3, w1_ref[...])).astype(BF16)
    new = (mid3.astype(F32) + dot(hidden, w2_ref[...])).astype(BF16)
    lower = coarse_parent(parent_ref, rows, level_three).T.astype(BF16)
    picked = dot(lower, new).astype(BF16)
    down = (mid_ref[...].astype(F32) + dot(picked, w_down_ref[...])).astype(BF16)
    down_ref[...] = down
    fine = dot(down, w_fine_ref[...]).astype(BF16)
    par_low, par_high = column_parts(par_ref[...])
    for j in range(par_ref.shape[0]):
        hot, high = lane_select(par_low[:, j : j + 1], par_high[:, j : j + 1])
        lower = jnp.concatenate([pick(hot, high, t) for t in range(fine.shape[0] // LANES)], axis=1)
        span = slice(j * LANES, (j + 1) * LANES)
        fine_out_ref[span] = (fine_ref[span].astype(F32) + dot(lower, fine)).astype(BF16)


def pair_slot():
    return lax.rem(lax.axis_index("wide") + lax.axis_index("core"), 2)


def quad_slot():
    return lax.rem(lax.axis_index("wide") + 2 * lax.axis_index("core"), 4)


def device_of(wide, chip, core):
    sizes = [lax.axis_size(name) for name in ("wide", "chip", "core")]
    return (wide % sizes[0] * sizes[1] + chip) * sizes[2] + core


def exchanged(value, groups):
    return lax.all_to_all(
        value, ("wide", "chip", "core"), 0, 0, tiled=True, axis_index_groups=groups
    )


def core_swapped(value):
    return lax.ppermute(value, "core", [(0, 1), (1, 0)])


def call(kernel, out, scratch=(), vmem=24, hbm=(), hbm_outs=False, nargs=0, flops=0, moved=0):
    specs = [
        pl.BlockSpec(memory_space=pl.ANY if k in hbm else pltpu.VMEM) for k in range(nargs)
    ]
    outs = [jax.ShapeDtypeStruct(shape, dtype) for shape, dtype in out]
    return pl.pallas_call(
        kernel,
        out_shape=outs,
        in_specs=specs,
        out_specs=[pl.BlockSpec(memory_space=pl.ANY if hbm_outs else pltpu.VMEM) for _ in outs],
        scratch_shapes=list(scratch),
        compiler_params=pltpu.CompilerParams(vmem_limit_bytes=vmem * 2**20),
        cost_estimate=pl.CostEstimate(flops=flops, bytes_accessed=moved, transcendentals=0),
    )


def body(
    fine_state, l2_state, l3_state, boundary, senders, receivers, up_parent, l2_parent, msg_in,
    msg_out, fine_gain, up_weight, l2_gain, l3_gain, l3_w1, l3_w2, down_weight, fine_down,
):
    nodes, width = fine_state.shape
    edges = senders.shape[0]
    level_two = l2_state.shape[0]
    level_three = l3_state.shape[0]
    wide = lax.axis_size("wide")
    rows = level_three // wide
    chips, cores = lax.axis_size("chip"), lax.axis_size("core")
    send = senders.reshape(-1, LANES)
    recv = receivers.reshape(-1, LANES)
    par = up_parent.reshape(-1, LANES)
    parent = l2_parent.reshape(-1, LANES)
    fine_gain, l2_gain, l3_gain = (g.reshape(1, width) for g in (fine_gain, l2_gain, l3_gain))

    hot = (boundary[:, None] == jnp.arange(nodes, dtype=jnp.int32)[None, :]).astype(BF16)
    exported = dot(hot, fine_state).astype(BF16)
    bound = chips * cores * boundary.shape[0]
    pairs = [
        [device_of(first + core + step, chip, core) for step in range(2) for chip in range(chips)]
        for core in range(cores)
        for first in range(0, wide, 2)
    ]
    quads = [
        [device_of(first + 2 * core + step, chip, core) for step in range(4)]
        for core in range(cores)
        for chip in range(chips)
        for first in range(0, wide, 4)
    ]

    (chip_rows,) = call(
        chip_rows_kernel, [((2 * chips, cores * boundary.shape[0], width), BF16)], nargs=2
    )(exported, core_swapped(exported))
    chip_rows, local_state = lax.optimization_barrier((chip_rows, fine_state))
    pair = exchanged(chip_rows, pairs).reshape(2, bound, width)

    pre, l3_rows = call(
        gather_kernel,
        [((edges, width), BF16), ((3 * rows, width), BF16)],
        [
            pltpu.VMEM((nodes, width), BF16),
            pltpu.VMEM((2 * width, width), BF16),
            pltpu.VMEM(send.shape, jnp.int32),
            pltpu.VMEM(recv.shape, jnp.int32),
            pltpu.VMEM((2 * nodes, width), BF16),
            pltpu.VMEM((edges, 2 * nodes), BF16),
            pltpu.VMEM((edges, width), BF16),
            pltpu.SemaphoreType.DMA((7 + edges // EDGE_BLOCK,)),
        ],
        hbm=range(5), hbm_outs=True, nargs=5, vmem=60, flops=5_000_000_000, moved=2_000_000,
    )(local_state, msg_in, send, recv, l3_state)
    pair, pre = lax.optimization_barrier((pair, pre))
    (near,) = call(neighbour_kernel, [((bound, width), BF16)], nargs=1)(pair)
    far = core_swapped(near)
    near, send_late = lax.optimization_barrier((near, send))
    hot, incidence = call(
        prepare_kernel, [((edges, 3 * bound), BF16), ((nodes, edges), BF16)],
        nargs=2, flops=1_000_000_000, moved=6_000_000,
    )(send_late, recv)
    far, hot, incidence = lax.optimization_barrier((far, hot, incidence))

    half = level_two // cores
    fine_mid, keep, give = call(
        fine_kernel,
        [((nodes, width), BF16), ((half, width), BF16), ((half, width), BF16)],
        [
            pltpu.VMEM((3 * bound, width), BF16),
            pltpu.VMEM((edges, width), BF16),
            pltpu.VMEM((level_two, width), F32),
        ],
        nargs=10, flops=3_000_000_000, moved=4_000_000,
    )(pre, pair, far, fine_state, hot, incidence, par, msg_in, msg_out, fine_gain)

    (chip_sums,) = call(add_kernel, [((chips, half, width), BF16)], nargs=2)(keep, core_swapped(give))
    chip_sums = lax.all_to_all(chip_sums, "chip", 0, 0, tiled=True)
    (half_mid,) = call(level_two_kernel, [((half, width), BF16)], nargs=4)(
        chip_sums, l2_state, up_weight, l2_gain
    )
    own, pieces, l2_mid = call(
        functools.partial(window_kernel, level_three),
        [((3 * rows, width), F32), ((4, 2 * rows, width), BF16), ((level_two, width), BF16)],
        [pltpu.VMEM((7 * rows, width), BF16)],
        nargs=3,
    )(half_mid, core_swapped(half_mid), parent)
    (mine,) = call(
        collect_kernel, [((3 * rows, width), BF16)], [pltpu.VMEM((3 * rows, width), F32)], nargs=1
    )(exchanged(pieces, quads))

    fine_out, l2_down = call(
        functools.partial(down_kernel, level_three),
        [((nodes, width), BF16), ((level_two, width), BF16)],
        nargs=13,
    )(
        own, mine, core_swapped(mine), l3_rows, l3_gain, l3_w1, l3_w2, down_weight, fine_down,
        parent, l2_mid, par, fine_mid,
    )
    return (fine_out, l2_down)


def solution(mesh):
    wide, narrow = mesh.devices.shape
    mesh = jax.sharding.Mesh(mesh.devices.reshape(wide, narrow // 2, 2), ("wide", "chip", "core"))
    every = ("wide", "chip", "core")
    return jax.shard_map(
        body,
        mesh=mesh,
        in_specs=(P(every, None), P("wide", None), P()) + (P(every),) * 4 + (P("wide"),) + (P(),) * 10,
        out_specs=(P(every, None), P("wide", None)),
        check_vma=False,
    )
```

```python
import functools

import jax
import jax.numpy as jnp
from jax import lax
from jax.experimental import pallas as pl
from jax.experimental.pallas import tpu as pltpu
from jax.sharding import PartitionSpec as P

F32 = jnp.float32
BF16 = jnp.bfloat16
LANES = 128
EDGE_BLOCK = 512


def dot(a, b):
    return jnp.dot(a, b, preferred_element_type=F32)


def rms_scale(values, gain):
    return values * lax.rsqrt(jnp.mean(values * values, axis=-1, keepdims=True) + 1e-05) * gain


def silu(x):
    half = 0.5 * x
    return half + half * jnp.tanh(half)


def column_parts(index):
    low = (index & (LANES - 1)).astype(F32)
    high = (index >> 7).astype(F32)
    return low.T, high.T


def lane_select(low_col, high_col):
    lane = lax.broadcasted_iota(jnp.int32, (LANES, LANES), 1).astype(F32)
    low = jnp.broadcast_to(low_col, (LANES, LANES))
    hot = jnp.where(low == lane, 1.0, 0.0).astype(BF16)
    high = jnp.broadcast_to(high_col, (LANES, LANES)).astype(BF16)
    return hot, high


def row_select(index_row):
    sub = lax.broadcasted_iota(jnp.int32, (LANES, LANES), 0)
    hot = jnp.where((index_row & (LANES - 1)) == sub, 1.0, 0.0).astype(BF16)
    high = jnp.broadcast_to((index_row >> 7).astype(F32), (LANES, LANES)).astype(BF16)
    return hot, high


def pick(hot, high, tile):
    return jnp.where(high == jnp.asarray(tile, BF16), hot, jnp.zeros_like(hot))


def gather_kernel(
    fs_hbm, w_in_hbm, send_hbm, recv_hbm, l3_hbm, pre_hbm, l3_rows_hbm,
    fs, w_in, send, recv, proj, hot, pre, sems,
):
    nodes, width = fs.shape
    edges = pre.shape[0]
    wide = lax.axis_index("wide")
    count = lax.axis_size("wide")
    rows = l3_rows_hbm.shape[0] // 3
    pairs = [(send_hbm, send), (recv_hbm, recv), (w_in_hbm, w_in), (fs_hbm, fs)]
    for k in range(3):
        block = lax.rem(wide + (k + count - 1), count)
        source = l3_hbm.at[pl.ds(pl.multiple_of(block * rows, rows), rows)]
        pairs.append((source, l3_rows_hbm.at[pl.ds(k * rows, rows)]))
    blocks = edges // EDGE_BLOCK
    for block in range(blocks):
        span = pl.ds(block * EDGE_BLOCK, EDGE_BLOCK)
        pairs.append((pre.at[span], pre_hbm.at[span]))
    copies = [pltpu.make_async_copy(a, b, sems.at[k]) for k, (a, b) in enumerate(pairs)]
    for copy in copies[:7]:
        copy.start()
    copies[0].wait()
    copies[1].wait()
    columns = [column_parts(send[...]), column_parts(recv[...])]
    for block in range(blocks):
        for part in range(EDGE_BLOCK // LANES):
            j = block * (EDGE_BLOCK // LANES) + part
            span = slice(j * LANES, (j + 1) * LANES)
            for side, (low, high) in enumerate(columns):
                hot_j, high_j = lane_select(low[:, j : j + 1], high[:, j : j + 1])
                for t in range(nodes // LANES):
                    start = side * nodes + t * LANES
                    hot[span, start : start + LANES] = pick(hot_j, high_j, t)
        if block == 0:
            copies[2].wait()
            copies[3].wait()
            proj[:nodes] = dot(fs[...], w_in[:width]).astype(BF16)
            proj[nodes:] = dot(fs[...], w_in[width:]).astype(BF16)
        span = slice(block * EDGE_BLOCK, (block + 1) * EDGE_BLOCK)
        pre[span] = dot(hot[span], proj[...]).astype(BF16)
        copies[7 + block].start()
    for copy in copies[4:]:
        copy.wait()


def chip_rows_kernel(mine_ref, other_ref, out_ref):
    rows = mine_ref.shape[0]
    core = lax.axis_index("core")
    first = jnp.where(core == 0, mine_ref[...], other_ref[...])
    last = jnp.where(core == 0, other_ref[...], mine_ref[...])
    for k in range(out_ref.shape[0]):
        out_ref[k, :rows] = first
        out_ref[k, rows:] = last


def neighbour_kernel(pair_ref, out_ref):
    out_ref[...] = pair_ref[1 - pair_slot()]


def prepare_kernel(send_ref, recv_ref, hot_ref, inc_ref):
    tiles = inc_ref.shape[0] // LANES
    low, high = column_parts(send_ref[...])
    for j in range(send_ref.shape[0]):
        span = slice(j * LANES, (j + 1) * LANES)
        hot_s, high_s = lane_select(low[:, j : j + 1], high[:, j : j + 1])
        for t in range(hot_ref.shape[1] // LANES):
            hot_ref[span, t * LANES : (t + 1) * LANES] = pick(hot_s, high_s, tiles + t)
        hot_r, high_r = row_select(recv_ref[j : j + 1])
        for t in range(tiles):
            inc_ref[t * LANES : (t + 1) * LANES, span] = pick(hot_r, high_r, t)


def fine_kernel(
    pre_ref, pair_ref, far_ref, fs_ref, hot_ref, inc_ref, par_ref, w_in_ref, w_out_ref, gain_ref,
    mid_ref, part_ref, around, agg, upper,
):
    nodes, width = fs_ref.shape
    edges = pre_ref.shape[0]
    tiles = nodes // LANES
    bound = far_ref.shape[0]
    slot = pair_slot()
    ahead = lax.rem(lax.axis_index("wide") + lax.axis_index("core"), 2) == 0
    near_at, far_at = jnp.where(ahead, 2 * bound, 0), jnp.where(ahead, 0, 2 * bound)
    around[pl.ds(pl.multiple_of(near_at, bound), bound)] = pair_ref[1 - slot]
    around[bound : 2 * bound] = pair_ref[slot]
    around[pl.ds(pl.multiple_of(far_at, bound), bound)] = far_ref[...]
    proj = dot(around[...], w_in_ref[:width]).astype(BF16)
    for j in range(tiles):
        hot_p, high_p = row_select(par_ref[j : j + 1])
        for t in range(upper.shape[0] // LANES):
            upper[t * LANES : (t + 1) * LANES, j * LANES : (j + 1) * LANES] = pick(hot_p, high_p, t)
    for block in range(edges // EDGE_BLOCK):
        span = slice(block * EDGE_BLOCK, (block + 1) * EDGE_BLOCK)
        hidden = silu(pre_ref[span].astype(F32) + dot(hot_ref[span], proj)).astype(BF16)
        for part in range(nodes // EDGE_BLOCK):
            here = slice(part * EDGE_BLOCK, (part + 1) * EDGE_BLOCK)
            more = dot(inc_ref[here, span], hidden)
            agg[here] = more if block == 0 else agg[here] + more
    for block in range(nodes // EDGE_BLOCK):
        span = slice(block * EDGE_BLOCK, (block + 1) * EDGE_BLOCK)
        summed = dot(agg[span].astype(BF16), w_out_ref[...])
        mid_ref[span] = (fs_ref[span].astype(F32) + rms_scale(summed, gain_ref[...])).astype(BF16)
    part_ref[...] = dot(upper[...], mid_ref[...]).astype(BF16)


def add_kernel(a_ref, b_ref, out_ref):
    total = (a_ref[...].astype(F32) + b_ref[...].astype(F32)).astype(BF16)
    for k in range(out_ref.shape[0]):
        out_ref[k] = total


def coarse_parent(parent_ref, rows, level_three):
    start = (lax.axis_index("wide") - 1) * rows
    local = (parent_ref[...] - start) & (level_three - 1)
    sub = lax.broadcasted_iota(jnp.int32, (3 * rows, LANES), 0)
    return jnp.concatenate(
        [jnp.where(local[j : j + 1] == sub, 1.0, 0.0) for j in range(parent_ref.shape[0])], axis=1
    )


def window_kernel(
    level_three, parts_ref, state_ref, w_up_ref, gain_ref, parent_ref,
    own_ref, pieces_ref, mid_ref, padded,
):
    rows = own_ref.shape[0] // 3
    core = lax.axis_index("core")
    total = parts_ref[0].astype(F32)
    for k in range(1, parts_ref.shape[0]):
        total = total + parts_ref[k].astype(F32)
    level = dot(total.astype(BF16), w_up_ref[...])
    mid = (state_ref[...].astype(F32) + rms_scale(level, gain_ref[...])).astype(BF16)
    mid_ref[...] = mid
    own = dot(coarse_parent(parent_ref, rows, level_three).astype(BF16), mid)
    own_ref[...] = own
    padded[...] = jnp.zeros_like(padded)
    padded[rows : 4 * rows] = own.astype(BF16)
    here = quad_slot()
    for there in range(pieces_ref.shape[0]):
        step = there - here
        start = jnp.where(
            step == 1, 2, jnp.where(step == 2, 3, jnp.where(step == -1, 1, jnp.where(step == -2, 0, 5)))
        )
        start = jnp.where((core == 1) & ((here >= 2) == (there >= 2)), 5, start)
        pieces_ref[there] = padded[pl.ds(pl.multiple_of(start * rows, rows), 2 * rows)]


def collect_kernel(pieces_ref, out_ref, sums):
    rows = out_ref.shape[0] // 3
    sums[...] = jnp.zeros_like(sums)
    here = quad_slot()
    for there in range(pieces_ref.shape[0]):
        start = pl.multiple_of(jnp.where(there < here, 0, rows), rows)
        sums[pl.ds(start, 2 * rows)] += pieces_ref[there].astype(F32)
    out_ref[...] = sums[...].astype(BF16)


def down_kernel(
    level_three, own_ref, mine_ref, other_ref, l3_rows_ref, gain_ref,
    w1_ref, w2_ref, w_down_ref, w_fine_ref, parent_ref, mid_ref, par_ref, fine_ref,
    fine_out_ref, down_ref,
):
    rows = own_ref.shape[0] // 3
    total = own_ref[...] + (mine_ref[...].astype(F32) + other_ref[...].astype(F32))
    mid3 = (l3_rows_ref[...].astype(F32) + rms_scale(total, gain_ref[...])).astype(BF16)
    hidden = silu(dot(mid3, w1_ref[...])).astype(BF16)
    new = (mid3.astype(F32) + dot(hidden, w2_ref[...])).astype(BF16)
    lower = coarse_parent(parent_ref, rows, level_three).T.astype(BF16)
    picked = dot(lower, new).astype(BF16)
    down = (mid_ref[...].astype(F32) + dot(picked, w_down_ref[...])).astype(BF16)
    down_ref[...] = down
    fine = dot(down, w_fine_ref[...]).astype(BF16)
    par_low, par_high = column_parts(par_ref[...])
    for j in range(par_ref.shape[0]):
        hot, high = lane_select(par_low[:, j : j + 1], par_high[:, j : j + 1])
        lower = jnp.concatenate([pick(hot, high, t) for t in range(fine.shape[0] // LANES)], axis=1)
        span = slice(j * LANES, (j + 1) * LANES)
        fine_out_ref[span] = (fine_ref[span].astype(F32) + dot(lower, fine)).astype(BF16)


def pair_slot():
    return lax.rem(lax.axis_index("wide") + lax.axis_index("core"), 2)


def quad_slot():
    return lax.rem(lax.axis_index("wide") + 2 * lax.axis_index("core"), 4)


def device_of(wide, chip, core):
    sizes = [lax.axis_size(name) for name in ("wide", "chip", "core")]
    return (wide % sizes[0] * sizes[1] + chip) * sizes[2] + core


def exchanged(value, groups):
    return lax.all_to_all(
        value, ("wide", "chip", "core"), 0, 0, tiled=True, axis_index_groups=groups
    )


def core_swapped(value):
    return lax.ppermute(value, "core", [(0, 1), (1, 0)])


def call(kernel, out, scratch=(), vmem=24, hbm=(), hbm_outs=False, nargs=0, flops=0, moved=0):
    specs = [
        pl.BlockSpec(memory_space=pl.ANY if k in hbm else pltpu.VMEM) for k in range(nargs)
    ]
    outs = [jax.ShapeDtypeStruct(shape, dtype) for shape, dtype in out]
    return pl.pallas_call(
        kernel,
        out_shape=outs,
        in_specs=specs,
        out_specs=[pl.BlockSpec(memory_space=pl.ANY if hbm_outs else pltpu.VMEM) for _ in outs],
        scratch_shapes=list(scratch),
        compiler_params=pltpu.CompilerParams(vmem_limit_bytes=vmem * 2**20),
        cost_estimate=pl.CostEstimate(flops=flops, bytes_accessed=moved, transcendentals=0),
    )


def body(
    fine_state, l2_state, l3_state, boundary, senders, receivers, up_parent, l2_parent, msg_in,
    msg_out, fine_gain, up_weight, l2_gain, l3_gain, l3_w1, l3_w2, down_weight, fine_down,
):
    nodes, width = fine_state.shape
    edges = senders.shape[0]
    level_two = l2_state.shape[0]
    level_three = l3_state.shape[0]
    wide = lax.axis_size("wide")
    rows = level_three // wide
    chips, cores = lax.axis_size("chip"), lax.axis_size("core")
    send = senders.reshape(-1, LANES)
    recv = receivers.reshape(-1, LANES)
    par = up_parent.reshape(-1, LANES)
    parent = l2_parent.reshape(-1, LANES)
    fine_gain, l2_gain, l3_gain = (g.reshape(1, width) for g in (fine_gain, l2_gain, l3_gain))

    hot = (boundary[:, None] == jnp.arange(nodes, dtype=jnp.int32)[None, :]).astype(BF16)
    exported = dot(hot, fine_state).astype(BF16)
    bound = chips * cores * boundary.shape[0]
    pairs = [
        [device_of(first + core + step, chip, core) for step in range(2) for chip in range(chips)]
        for core in range(cores)
        for first in range(0, wide, 2)
    ]
    quads = [
        [device_of(first + 2 * core + step, chip, core) for step in range(4)]
        for core in range(cores)
        for chip in range(chips)
        for first in range(0, wide, 4)
    ]

    (chip_rows,) = call(
        chip_rows_kernel, [((2 * chips, cores * boundary.shape[0], width), BF16)], nargs=2
    )(exported, core_swapped(exported))
    chip_rows, local_state = lax.optimization_barrier((chip_rows, fine_state))
    pair = exchanged(chip_rows, pairs).reshape(2, bound, width)

    pre, l3_rows = call(
        gather_kernel,
        [((edges, width), BF16), ((3 * rows, width), BF16)],
        [
            pltpu.VMEM((nodes, width), BF16),
            pltpu.VMEM((2 * width, width), BF16),
            pltpu.VMEM(send.shape, jnp.int32),
            pltpu.VMEM(recv.shape, jnp.int32),
            pltpu.VMEM((2 * nodes, width), BF16),
            pltpu.VMEM((edges, 2 * nodes), BF16),
            pltpu.VMEM((edges, width), BF16),
            pltpu.SemaphoreType.DMA((7 + edges // EDGE_BLOCK,)),
        ],
        hbm=range(5), hbm_outs=True, nargs=5, vmem=60, flops=5_000_000_000, moved=2_000_000,
    )(local_state, msg_in, send, recv, l3_state)
    pair, pre = lax.optimization_barrier((pair, pre))
    (near,) = call(neighbour_kernel, [((bound, width), BF16)], nargs=1)(pair)
    far = core_swapped(near)
    near, send_late = lax.optimization_barrier((near, send))
    hot, incidence = call(
        prepare_kernel, [((edges, 3 * bound), BF16), ((nodes, edges), BF16)],
        nargs=2, flops=1_000_000_000, moved=6_000_000,
    )(send_late, recv)
    far, hot, incidence = lax.optimization_barrier((far, hot, incidence))

    fine_mid, part = call(
        fine_kernel,
        [((nodes, width), BF16), ((level_two, width), BF16)],
        [
            pltpu.VMEM((3 * bound, width), BF16),
            pltpu.VMEM((nodes, width), F32),
            pltpu.VMEM((level_two, nodes), BF16),
        ],
        nargs=10, flops=3_000_000_000, moved=4_000_000,
    )(pre, pair, far, fine_state, hot, incidence, par, msg_in, msg_out, fine_gain)

    (chip_sums,) = call(add_kernel, [((chips, level_two, width), BF16)], nargs=2)(
        part, core_swapped(part)
    )
    chip_sums = lax.all_to_all(chip_sums, "chip", 0, 0, tiled=True)
    own, pieces, l2_mid = call(
        functools.partial(window_kernel, level_three),
        [((3 * rows, width), F32), ((4, 2 * rows, width), BF16), ((level_two, width), BF16)],
        [pltpu.VMEM((7 * rows, width), BF16)],
        nargs=5,
    )(chip_sums, l2_state, up_weight, l2_gain, parent)
    (mine,) = call(
        collect_kernel, [((3 * rows, width), BF16)], [pltpu.VMEM((3 * rows, width), F32)], nargs=1
    )(exchanged(pieces, quads))

    fine_out, l2_down = call(
        functools.partial(down_kernel, level_three),
        [((nodes, width), BF16), ((level_two, width), BF16)],
        nargs=13,
    )(
        own, mine, core_swapped(mine), l3_rows, l3_gain, l3_w1, l3_w2, down_weight, fine_down,
        parent, l2_mid, par, fine_mid,
    )
    return (fine_out, l2_down)


def solution(mesh):
    wide, narrow = mesh.devices.shape
    mesh = jax.sharding.Mesh(mesh.devices.reshape(wide, narrow // 2, 2), ("wide", "chip", "core"))
    every = ("wide", "chip", "core")
    return jax.shard_map(
        body,
        mesh=mesh,
        in_specs=(P(every, None), P("wide", None), P()) + (P(every),) * 4 + (P("wide"),) + (P(),) * 10,
        out_specs=(P(every, None), P("wide", None)),
        check_vma=False,
    )
```

```python
import functools

import jax
import jax.numpy as jnp
from jax import lax
from jax.experimental import pallas as pl
from jax.experimental.pallas import tpu as pltpu
from jax.sharding import PartitionSpec as P

F32 = jnp.float32
BF16 = jnp.bfloat16
LANES = 128
EDGE_BLOCK = 512


def dot(a, b):
    return jnp.dot(a, b, preferred_element_type=F32)


def rms_scale(values, gain):
    return values * lax.rsqrt(jnp.mean(values * values, axis=-1, keepdims=True) + 1e-05) * gain


def silu(x):
    half = 0.5 * x
    return half + half * jnp.tanh(half)


def column_parts(*indices):
    parts = []
    for index in indices:
        parts.append((index & (LANES - 1)).astype(F32))
        parts.append((index >> 7).astype(F32))
    columns = jnp.concatenate(parts, axis=0).T
    out, start = [], 0
    for index in indices:
        k = index.shape[0]
        out.append((columns[:, start : start + k], columns[:, start + k : start + 2 * k]))
        start += 2 * k
    return out


def lane_select(low_col, high_col):
    lane = lax.broadcasted_iota(jnp.int32, (LANES, LANES), 1).astype(F32)
    low = jnp.broadcast_to(low_col, (LANES, LANES))
    hot = jnp.where(low == lane, 1.0, 0.0).astype(BF16)
    high = jnp.broadcast_to(high_col, (LANES, LANES)).astype(BF16)
    return hot, high


def row_select(index_row):
    sub = lax.broadcasted_iota(jnp.int32, (LANES, LANES), 0)
    hot = jnp.where((index_row & (LANES - 1)) == sub, 1.0, 0.0).astype(BF16)
    high = jnp.broadcast_to((index_row >> 7).astype(F32), (LANES, LANES)).astype(BF16)
    return hot, high


def pick(hot, high, tile):
    return jnp.where(high == jnp.asarray(tile, BF16), hot, jnp.zeros_like(hot))


def gather_kernel(
    fs_hbm, w_in_hbm, send_hbm, recv_hbm, l3_hbm, pre_hbm, l3_rows_hbm,
    fs, w_in, send, recv, proj, hot, pre, sems,
):
    nodes, width = fs.shape
    edges = pre.shape[0]
    wide = lax.axis_index("wide")
    count = lax.axis_size("wide")
    rows = l3_rows_hbm.shape[0] // 3
    pairs = [(send_hbm, send), (recv_hbm, recv), (w_in_hbm, w_in)]
    quarter = nodes // 4
    for k in range(4):
        pairs.append((fs_hbm.at[pl.ds(k * quarter, quarter)], fs.at[pl.ds(k * quarter, quarter)]))
    for k in range(3):
        block = lax.rem(wide + (k + count - 1), count)
        source = l3_hbm.at[pl.ds(pl.multiple_of(block * rows, rows), rows)]
        pairs.append((source, l3_rows_hbm.at[pl.ds(k * rows, rows)]))
    blocks = edges // EDGE_BLOCK
    for block in range(blocks):
        span = pl.ds(block * EDGE_BLOCK, EDGE_BLOCK)
        pairs.append((pre.at[span], pre_hbm.at[span]))
    copies = [pltpu.make_async_copy(a, b, sems.at[k]) for k, (a, b) in enumerate(pairs)]
    for copy in copies[:10]:
        copy.start()
    copies[0].wait()
    copies[1].wait()
    columns = column_parts(send[...], recv[...])
    for block in range(blocks):
        for part in range(EDGE_BLOCK // LANES):
            j = block * (EDGE_BLOCK // LANES) + part
            span = slice(j * LANES, (j + 1) * LANES)
            for side, (low, high) in enumerate(columns):
                hot_j, high_j = lane_select(low[:, j : j + 1], high[:, j : j + 1])
                for t in range(nodes // LANES):
                    start = side * nodes + t * LANES
                    hot[span, start : start + LANES] = pick(hot_j, high_j, t)
        if block == 0:
            copies[2].wait()
            for k in range(4):
                copies[3 + k].wait()
                rows_in = fs[k * quarter : (k + 1) * quarter]
                for side in range(2):
                    start = side * nodes + k * quarter
                    proj[start : start + quarter] = dot(
                        rows_in, w_in[side * width : (side + 1) * width]
                    ).astype(BF16)
        span = slice(block * EDGE_BLOCK, (block + 1) * EDGE_BLOCK)
        pre[span] = dot(hot[span], proj[...]).astype(BF16)
        copies[10 + block].start()
    for copy in copies[7:]:
        copy.wait()


def chip_rows_kernel(mine_ref, other_ref, out_ref):
    rows = mine_ref.shape[0]
    core = lax.axis_index("core")
    first = jnp.where(core == 0, mine_ref[...], other_ref[...])
    last = jnp.where(core == 0, other_ref[...], mine_ref[...])
    for k in range(out_ref.shape[0]):
        out_ref[k, :rows] = first
        out_ref[k, rows:] = last


def neighbour_kernel(pair_ref, out_ref):
    out_ref[...] = pair_ref[1 - pair_slot()]


def incidence_kernel(recv_ref, inc_ref):
    for j in range(recv_ref.shape[0]):
        hot, high = row_select(recv_ref[j : j + 1])
        for t in range(inc_ref.shape[0] // LANES):
            inc_ref[t * LANES : (t + 1) * LANES, j * LANES : (j + 1) * LANES] = pick(hot, high, t)


def fine_kernel(
    pre_ref, pair_ref, far_ref, fs_ref, send_ref, inc_ref, par_ref, w_in_ref, w_out_ref, gain_ref,
    mid_ref, part_ref, around, agg, upper, hot,
):
    nodes, width = fs_ref.shape
    edges = pre_ref.shape[0]
    tiles = nodes // LANES
    bound = far_ref.shape[0]
    slot = pair_slot()
    ahead = lax.rem(lax.axis_index("wide") + lax.axis_index("core"), 2) == 0
    near_at, far_at = jnp.where(ahead, 2 * bound, 0), jnp.where(ahead, 0, 2 * bound)
    around[pl.ds(pl.multiple_of(near_at, bound), bound)] = pair_ref[1 - slot]
    around[bound : 2 * bound] = pair_ref[slot]
    around[pl.ds(pl.multiple_of(far_at, bound), bound)] = far_ref[...]
    proj = dot(around[...], w_in_ref[:width]).astype(BF16)
    ((low, high),) = column_parts(send_ref[...])
    for j in range(tiles):
        hot_p, high_p = row_select(par_ref[j : j + 1])
        for t in range(upper.shape[0] // LANES):
            upper[t * LANES : (t + 1) * LANES, j * LANES : (j + 1) * LANES] = pick(hot_p, high_p, t)
    for block in range(edges // EDGE_BLOCK):
        span = slice(block * EDGE_BLOCK, (block + 1) * EDGE_BLOCK)
        for j in range(block * EDGE_BLOCK // LANES, (block + 1) * EDGE_BLOCK // LANES):
            hot_s, high_s = lane_select(low[:, j : j + 1], high[:, j : j + 1])
            for t in range(hot.shape[1] // LANES):
                hot[j * LANES : (j + 1) * LANES, t * LANES : (t + 1) * LANES] = pick(
                    hot_s, high_s, tiles + t
                )
        hidden = silu(pre_ref[span].astype(F32) + dot(hot[span], proj)).astype(BF16)
        for part in range(nodes // EDGE_BLOCK):
            here = slice(part * EDGE_BLOCK, (part + 1) * EDGE_BLOCK)
            more = dot(inc_ref[here, span], hidden)
            agg[here] = more if block == 0 else agg[here] + more
    for block in range(nodes // EDGE_BLOCK):
        span = slice(block * EDGE_BLOCK, (block + 1) * EDGE_BLOCK)
        summed = dot(agg[span].astype(BF16), w_out_ref[...])
        mid_ref[span] = (fs_ref[span].astype(F32) + rms_scale(summed, gain_ref[...])).astype(BF16)
    part_ref[...] = dot(upper[...], mid_ref[...]).astype(BF16)


def add_kernel(a_ref, b_ref, out_ref):
    total = (a_ref[...].astype(F32) + b_ref[...].astype(F32)).astype(BF16)
    for k in range(out_ref.shape[0]):
        out_ref[k] = total


def coarse_parent(parent_ref, rows, level_three):
    start = (lax.axis_index("wide") - 1) * rows
    local = (parent_ref[...] - start) & (level_three - 1)
    sub = lax.broadcasted_iota(jnp.int32, (3 * rows, LANES), 0)
    return jnp.concatenate(
        [jnp.where(local[j : j + 1] == sub, 1.0, 0.0) for j in range(parent_ref.shape[0])], axis=1
    )


def window_kernel(
    level_three, parts_ref, state_ref, w_up_ref, gain_ref, parent_ref,
    own_ref, pieces_ref, mid_ref, padded,
):
    rows = own_ref.shape[0] // 3
    core = lax.axis_index("core")
    total = parts_ref[0].astype(F32)
    for k in range(1, parts_ref.shape[0]):
        total = total + parts_ref[k].astype(F32)
    level = dot(total.astype(BF16), w_up_ref[...])
    mid = (state_ref[...].astype(F32) + rms_scale(level, gain_ref[...])).astype(BF16)
    mid_ref[...] = mid
    own = dot(coarse_parent(parent_ref, rows, level_three).astype(BF16), mid)
    own_ref[...] = own
    padded[...] = jnp.zeros_like(padded)
    padded[rows : 4 * rows] = own.astype(BF16)
    here = quad_slot()
    for there in range(pieces_ref.shape[0]):
        step = there - here
        start = jnp.where(
            step == 1, 2, jnp.where(step == 2, 3, jnp.where(step == -1, 1, jnp.where(step == -2, 0, 5)))
        )
        start = jnp.where((core == 1) & ((here >= 2) == (there >= 2)), 5, start)
        pieces_ref[there] = padded[pl.ds(pl.multiple_of(start * rows, rows), 2 * rows)]


def collect_kernel(pieces_ref, out_ref, sums):
    rows = out_ref.shape[0] // 3
    sums[...] = jnp.zeros_like(sums)
    here = quad_slot()
    for there in range(pieces_ref.shape[0]):
        start = pl.multiple_of(jnp.where(there < here, 0, rows), rows)
        sums[pl.ds(start, 2 * rows)] += pieces_ref[there].astype(F32)
    out_ref[...] = sums[...].astype(BF16)


def down_kernel(
    level_three, own_ref, mine_ref, other_ref, l3_rows_ref, gain_ref,
    w1_ref, w2_ref, w_down_ref, w_fine_ref, parent_ref, mid_ref, par_ref, fine_ref,
    fine_out_hbm, down_hbm, fine_out, down_out, sems,
):
    rows = own_ref.shape[0] // 3
    total = own_ref[...] + (mine_ref[...].astype(F32) + other_ref[...].astype(F32))
    mid3 = (l3_rows_ref[...].astype(F32) + rms_scale(total, gain_ref[...])).astype(BF16)
    hidden = silu(dot(mid3, w1_ref[...])).astype(BF16)
    new = (mid3.astype(F32) + dot(hidden, w2_ref[...])).astype(BF16)
    lower = coarse_parent(parent_ref, rows, level_three).T.astype(BF16)
    picked = dot(lower, new).astype(BF16)
    down = (mid_ref[...].astype(F32) + dot(picked, w_down_ref[...])).astype(BF16)
    down_out[...] = down
    copies = [pltpu.make_async_copy(down_out, down_hbm, sems.at[0])]
    copies[0].start()
    fine = dot(down, w_fine_ref[...]).astype(BF16)
    ((par_low, par_high),) = column_parts(par_ref[...])
    for j in range(par_ref.shape[0]):
        hot, high = lane_select(par_low[:, j : j + 1], par_high[:, j : j + 1])
        lower = jnp.concatenate([pick(hot, high, t) for t in range(fine.shape[0] // LANES)], axis=1)
        span = slice(j * LANES, (j + 1) * LANES)
        fine_out[span] = (fine_ref[span].astype(F32) + dot(lower, fine)).astype(BF16)
        if j % 2 == 1:
            part = pl.ds((j - 1) * LANES, 2 * LANES)
            copies.append(
                pltpu.make_async_copy(fine_out.at[part], fine_out_hbm.at[part], sems.at[(j + 1) // 2])
            )
            copies[-1].start()
    for copy in copies:
        copy.wait()


def pair_slot():
    return lax.rem(lax.axis_index("wide") + lax.axis_index("core"), 2)


def quad_slot():
    return lax.rem(lax.axis_index("wide") + 2 * lax.axis_index("core"), 4)


def device_of(wide, chip, core):
    sizes = [lax.axis_size(name) for name in ("wide", "chip", "core")]
    return (wide % sizes[0] * sizes[1] + chip) * sizes[2] + core


def exchanged(value, groups):
    return lax.all_to_all(
        value, ("wide", "chip", "core"), 0, 0, tiled=True, axis_index_groups=groups
    )


def core_swapped(value):
    return lax.ppermute(value, "core", [(0, 1), (1, 0)])


def call(kernel, out, scratch=(), vmem=24, hbm=(), hbm_outs=False, nargs=0, flops=0, moved=0):
    specs = [
        pl.BlockSpec(memory_space=pl.ANY if k in hbm else pltpu.VMEM) for k in range(nargs)
    ]
    outs = [jax.ShapeDtypeStruct(shape, dtype) for shape, dtype in out]
    return pl.pallas_call(
        kernel,
        out_shape=outs,
        in_specs=specs,
        out_specs=[pl.BlockSpec(memory_space=pl.ANY if hbm_outs else pltpu.VMEM) for _ in outs],
        scratch_shapes=list(scratch),
        compiler_params=pltpu.CompilerParams(vmem_limit_bytes=vmem * 2**20),
        cost_estimate=pl.CostEstimate(flops=flops, bytes_accessed=moved, transcendentals=0),
    )


def body(
    fine_state, l2_state, l3_state, boundary, senders, receivers, up_parent, l2_parent, msg_in,
    msg_out, fine_gain, up_weight, l2_gain, l3_gain, l3_w1, l3_w2, down_weight, fine_down,
):
    nodes, width = fine_state.shape
    edges = senders.shape[0]
    level_two = l2_state.shape[0]
    level_three = l3_state.shape[0]
    wide = lax.axis_size("wide")
    rows = level_three // wide
    chips, cores = lax.axis_size("chip"), lax.axis_size("core")
    send = senders.reshape(-1, LANES)
    recv = receivers.reshape(-1, LANES)
    par = up_parent.reshape(-1, LANES)
    parent = l2_parent.reshape(-1, LANES)
    fine_gain, l2_gain, l3_gain = (g.reshape(1, width) for g in (fine_gain, l2_gain, l3_gain))

    hot = (boundary[:, None] == jnp.arange(nodes, dtype=jnp.int32)[None, :]).astype(BF16)
    exported = dot(hot, fine_state).astype(BF16)
    bound = chips * cores * boundary.shape[0]
    pairs = [
        [device_of(first + core + step, chip, core) for step in range(2) for chip in range(chips)]
        for core in range(cores)
        for first in range(0, wide, 2)
    ]
    quads = [
        [device_of(first + 2 * core + step, chip, core) for step in range(4)]
        for core in range(cores)
        for chip in range(chips)
        for first in range(0, wide, 4)
    ]

    (chip_rows,) = call(
        chip_rows_kernel, [((2 * chips, cores * boundary.shape[0], width), BF16)], nargs=2
    )(exported, core_swapped(exported))
    chip_rows, local_state = lax.optimization_barrier((chip_rows, fine_state))
    pair = exchanged(chip_rows, pairs).reshape(2, bound, width)

    pre, l3_rows = call(
        gather_kernel,
        [((edges, width), BF16), ((3 * rows, width), BF16)],
        [
            pltpu.VMEM((nodes, width), BF16),
            pltpu.VMEM((2 * width, width), BF16),
            pltpu.VMEM(send.shape, jnp.int32),
            pltpu.VMEM(recv.shape, jnp.int32),
            pltpu.VMEM((2 * nodes, width), BF16),
            pltpu.VMEM((edges, 2 * nodes), BF16),
            pltpu.VMEM((edges, width), BF16),
            pltpu.SemaphoreType.DMA((10 + edges // EDGE_BLOCK,)),
        ],
        hbm=range(5), hbm_outs=True, nargs=5, vmem=60, flops=5_000_000_000, moved=2_000_000,
    )(local_state, msg_in, send, recv, l3_state)
    pair, pre = lax.optimization_barrier((pair, pre))
    (near,) = call(neighbour_kernel, [((bound, width), BF16)], nargs=1)(pair)
    far = core_swapped(near)
    near, recv_late = lax.optimization_barrier((near, recv))
    (incidence,) = call(
        incidence_kernel, [((nodes, edges), BF16)],
        nargs=1, flops=1_000_000_000, moved=4_000_000,
    )(recv_late)
    far, incidence = lax.optimization_barrier((far, incidence))

    fine_mid, part = call(
        fine_kernel,
        [((nodes, width), BF16), ((level_two, width), BF16)],
        [
            pltpu.VMEM((3 * bound, width), BF16),
            pltpu.VMEM((nodes, width), F32),
            pltpu.VMEM((level_two, nodes), BF16),
            pltpu.VMEM((edges, 3 * bound), BF16),
        ],
        nargs=10, flops=3_000_000_000, moved=4_000_000,
    )(pre, pair, far, fine_state, send, incidence, par, msg_in, msg_out, fine_gain)

    (chip_sums,) = call(add_kernel, [((chips, level_two, width), BF16)], nargs=2)(
        part, core_swapped(part)
    )
    chip_sums = lax.all_to_all(chip_sums, "chip", 0, 0, tiled=True)
    own, pieces, l2_mid = call(
        functools.partial(window_kernel, level_three),
        [((3 * rows, width), F32), ((4, 2 * rows, width), BF16), ((level_two, width), BF16)],
        [pltpu.VMEM((7 * rows, width), BF16)],
        nargs=5,
    )(chip_sums, l2_state, up_weight, l2_gain, parent)
    (mine,) = call(
        collect_kernel, [((3 * rows, width), BF16)], [pltpu.VMEM((3 * rows, width), F32)], nargs=1
    )(exchanged(pieces, quads))

    fine_out, l2_down = call(
        functools.partial(down_kernel, level_three),
        [((nodes, width), BF16), ((level_two, width), BF16)],
        [
            pltpu.VMEM((nodes, width), BF16),
            pltpu.VMEM((level_two, width), BF16),
            pltpu.SemaphoreType.DMA((1 + nodes // (2 * LANES),)),
        ],
        nargs=13, hbm_outs=True,
    )(
        own, mine, core_swapped(mine), l3_rows, l3_gain, l3_w1, l3_w2, down_weight, fine_down,
        parent, l2_mid, par, fine_mid,
    )
    return (fine_out, l2_down)


def solution(mesh):
    wide, narrow = mesh.devices.shape
    mesh = jax.sharding.Mesh(mesh.devices.reshape(wide, narrow // 2, 2), ("wide", "chip", "core"))
    every = ("wide", "chip", "core")
    return jax.shard_map(
        body,
        mesh=mesh,
        in_specs=(P(every, None), P("wide", None), P()) + (P(every),) * 4 + (P("wide"),) + (P(),) * 10,
        out_specs=(P(every, None), P("wide", None)),
        check_vma=False,
    )
```

```python
import functools

import jax
import jax.numpy as jnp
from jax import lax
from jax.experimental import pallas as pl
from jax.experimental.pallas import tpu as pltpu
from jax.sharding import PartitionSpec as P

F32 = jnp.float32
BF16 = jnp.bfloat16
LANES = 128
EDGE_BLOCK = 512


def dot(a, b):
    return jnp.dot(a, b, preferred_element_type=F32)


def rms_scale(values, gain):
    return values * lax.rsqrt(jnp.mean(values * values, axis=-1, keepdims=True) + 1e-05) * gain


def silu(x):
    half = 0.5 * x
    return half + half * jnp.tanh(half)


def column_parts(*indices):
    parts = []
    for index in indices:
        parts.append((index & (LANES - 1)).astype(F32))
        parts.append((index >> 7).astype(F32))
    columns = jnp.concatenate(parts, axis=0).T
    out, start = [], 0
    for index in indices:
        k = index.shape[0]
        out.append((columns[:, start : start + k], columns[:, start + k : start + 2 * k]))
        start += 2 * k
    return out


def lane_select(low_col, high_col):
    lane = lax.broadcasted_iota(jnp.int32, (LANES, LANES), 1).astype(F32)
    low = jnp.broadcast_to(low_col, (LANES, LANES))
    hot = jnp.where(low == lane, 1.0, 0.0).astype(BF16)
    high = jnp.broadcast_to(high_col, (LANES, LANES)).astype(BF16)
    return hot, high


def row_select(index_row):
    sub = lax.broadcasted_iota(jnp.int32, (LANES, LANES), 0)
    hot = jnp.where((index_row & (LANES - 1)) == sub, 1.0, 0.0).astype(BF16)
    high = jnp.broadcast_to((index_row >> 7).astype(F32), (LANES, LANES)).astype(BF16)
    return hot, high


def pick(hot, high, tile):
    return jnp.where(high == jnp.asarray(tile, BF16), hot, jnp.zeros_like(hot))


def gather_kernel(fs_ref, w_in_ref, send_ref, recv_ref, pre_ref, proj, hot):
    nodes, width = fs_ref.shape
    edges = pre_ref.shape[0]
    proj[:nodes] = dot(fs_ref[...], w_in_ref[:width]).astype(BF16)
    proj[nodes:] = dot(fs_ref[...], w_in_ref[width:]).astype(BF16)
    columns = column_parts(send_ref[...], recv_ref[...])
    for block in range(edges // EDGE_BLOCK):
        for part in range(EDGE_BLOCK // LANES):
            j = block * (EDGE_BLOCK // LANES) + part
            span = slice(j * LANES, (j + 1) * LANES)
            for side, (low, high) in enumerate(columns):
                hot_j, high_j = lane_select(low[:, j : j + 1], high[:, j : j + 1])
                for t in range(nodes // LANES):
                    start = side * nodes + t * LANES
                    hot[span, start : start + LANES] = pick(hot_j, high_j, t)
        span = slice(block * EDGE_BLOCK, (block + 1) * EDGE_BLOCK)
        pre_ref[span] = dot(hot[span], proj[...]).astype(BF16)


def chip_rows_kernel(mine_ref, other_ref, out_ref):
    rows = mine_ref.shape[0]
    core = lax.axis_index("core")
    first = jnp.where(core == 0, mine_ref[...], other_ref[...])
    last = jnp.where(core == 0, other_ref[...], mine_ref[...])
    for k in range(out_ref.shape[0]):
        out_ref[k, :rows] = first
        out_ref[k, rows:] = last


def neighbour_kernel(pair_ref, out_ref):
    out_ref[...] = pair_ref[1 - pair_slot()]


def incidence_kernel(recv_ref, inc_ref):
    for j in range(recv_ref.shape[0]):
        hot, high = row_select(recv_ref[j : j + 1])
        for t in range(inc_ref.shape[0] // LANES):
            inc_ref[t * LANES : (t + 1) * LANES, j * LANES : (j + 1) * LANES] = pick(hot, high, t)


def fine_kernel(
    pre_ref, pair_ref, far_ref, fs_ref, send_ref, inc_ref, par_ref, w_in_ref, w_out_ref, gain_ref,
    mid_ref, part_ref, around, agg, upper, hot,
):
    nodes, width = fs_ref.shape
    edges = pre_ref.shape[0]
    tiles = nodes // LANES
    bound = far_ref.shape[0]
    slot = pair_slot()
    ahead = lax.rem(lax.axis_index("wide") + lax.axis_index("core"), 2) == 0
    near_at, far_at = jnp.where(ahead, 2 * bound, 0), jnp.where(ahead, 0, 2 * bound)
    around[pl.ds(pl.multiple_of(near_at, bound), bound)] = pair_ref[1 - slot]
    around[bound : 2 * bound] = pair_ref[slot]
    around[pl.ds(pl.multiple_of(far_at, bound), bound)] = far_ref[...]
    proj = dot(around[...], w_in_ref[:width]).astype(BF16)
    ((low, high),) = column_parts(send_ref[...])
    for j in range(tiles):
        hot_p, high_p = row_select(par_ref[j : j + 1])
        for t in range(upper.shape[0] // LANES):
            upper[t * LANES : (t + 1) * LANES, j * LANES : (j + 1) * LANES] = pick(hot_p, high_p, t)
    for block in range(edges // EDGE_BLOCK):
        span = slice(block * EDGE_BLOCK, (block + 1) * EDGE_BLOCK)
        for j in range(block * EDGE_BLOCK // LANES, (block + 1) * EDGE_BLOCK // LANES):
            hot_s, high_s = lane_select(low[:, j : j + 1], high[:, j : j + 1])
            for t in range(hot.shape[1] // LANES):
                hot[j * LANES : (j + 1) * LANES, t * LANES : (t + 1) * LANES] = pick(
                    hot_s, high_s, tiles + t
                )
        hidden = silu(pre_ref[span].astype(F32) + dot(hot[span], proj)).astype(BF16)
        for part in range(nodes // EDGE_BLOCK):
            here = slice(part * EDGE_BLOCK, (part + 1) * EDGE_BLOCK)
            more = dot(inc_ref[here, span], hidden)
            agg[here] = more if block == 0 else agg[here] + more
    for block in range(nodes // EDGE_BLOCK):
        span = slice(block * EDGE_BLOCK, (block + 1) * EDGE_BLOCK)
        summed = dot(agg[span].astype(BF16), w_out_ref[...])
        mid_ref[span] = (fs_ref[span].astype(F32) + rms_scale(summed, gain_ref[...])).astype(BF16)
    part_ref[...] = dot(upper[...], mid_ref[...]).astype(BF16)


def add_kernel(a_ref, b_ref, out_ref):
    total = (a_ref[...].astype(F32) + b_ref[...].astype(F32)).astype(BF16)
    for k in range(out_ref.shape[0]):
        out_ref[k] = total


def coarse_parent(parent_ref, rows, level_three):
    start = (lax.axis_index("wide") - 1) * rows
    local = (parent_ref[...] - start) & (level_three - 1)
    sub = lax.broadcasted_iota(jnp.int32, (3 * rows, LANES), 0)
    return jnp.concatenate(
        [jnp.where(local[j : j + 1] == sub, 1.0, 0.0) for j in range(parent_ref.shape[0])], axis=1
    )


def window_kernel(
    level_three, parts_ref, state_ref, w_up_ref, gain_ref, parent_ref, l3_hbm,
    own_ref, pieces_ref, mid_ref, l3_rows_ref, padded, sems,
):
    rows = own_ref.shape[0] // 3
    core = lax.axis_index("core")
    wide = lax.axis_index("wide")
    count = lax.axis_size("wide")
    copies = []
    for k in range(3):
        block = lax.rem(wide + (k + count - 1), count)
        copies.append(
            pltpu.make_async_copy(
                l3_hbm.at[pl.ds(pl.multiple_of(block * rows, rows), rows)],
                l3_rows_ref.at[pl.ds(k * rows, rows)],
                sems.at[k],
            )
        )
    for copy in copies:
        copy.start()
    total = parts_ref[0].astype(F32)
    for k in range(1, parts_ref.shape[0]):
        total = total + parts_ref[k].astype(F32)
    level = dot(total.astype(BF16), w_up_ref[...])
    mid = (state_ref[...].astype(F32) + rms_scale(level, gain_ref[...])).astype(BF16)
    mid_ref[...] = mid
    own = dot(coarse_parent(parent_ref, rows, level_three).astype(BF16), mid)
    own_ref[...] = own
    padded[...] = jnp.zeros_like(padded)
    padded[rows : 4 * rows] = own.astype(BF16)
    here = quad_slot()
    for there in range(pieces_ref.shape[0]):
        step = there - here
        start = jnp.where(
            step == 1, 2, jnp.where(step == 2, 3, jnp.where(step == -1, 1, jnp.where(step == -2, 0, 5)))
        )
        start = jnp.where((core == 1) & ((here >= 2) == (there >= 2)), 5, start)
        pieces_ref[there] = padded[pl.ds(pl.multiple_of(start * rows, rows), 2 * rows)]
    for copy in copies:
        copy.wait()


def collect_kernel(pieces_ref, out_ref, sums):
    rows = out_ref.shape[0] // 3
    sums[...] = jnp.zeros_like(sums)
    here = quad_slot()
    for there in range(pieces_ref.shape[0]):
        start = pl.multiple_of(jnp.where(there < here, 0, rows), rows)
        sums[pl.ds(start, 2 * rows)] += pieces_ref[there].astype(F32)
    out_ref[...] = sums[...].astype(BF16)


def down_kernel(
    level_three, own_ref, mine_ref, other_ref, l3_rows_ref, gain_ref,
    w1_ref, w2_ref, w_down_ref, w_fine_ref, parent_ref, mid_ref, par_ref, fine_ref,
    fine_out_hbm, down_hbm, fine_out, down_out, sems,
):
    rows = own_ref.shape[0] // 3
    total = own_ref[...] + (mine_ref[...].astype(F32) + other_ref[...].astype(F32))
    mid3 = (l3_rows_ref[...].astype(F32) + rms_scale(total, gain_ref[...])).astype(BF16)
    hidden = silu(dot(mid3, w1_ref[...])).astype(BF16)
    new = (mid3.astype(F32) + dot(hidden, w2_ref[...])).astype(BF16)
    lower = coarse_parent(parent_ref, rows, level_three).T.astype(BF16)
    picked = dot(lower, new).astype(BF16)
    down = (mid_ref[...].astype(F32) + dot(picked, w_down_ref[...])).astype(BF16)
    down_out[...] = down
    copies = [pltpu.make_async_copy(down_out, down_hbm, sems.at[0])]
    copies[0].start()
    fine = dot(down, w_fine_ref[...]).astype(BF16)
    ((par_low, par_high),) = column_parts(par_ref[...])
    for j in range(par_ref.shape[0]):
        hot, high = lane_select(par_low[:, j : j + 1], par_high[:, j : j + 1])
        lower = jnp.concatenate([pick(hot, high, t) for t in range(fine.shape[0] // LANES)], axis=1)
        span = slice(j * LANES, (j + 1) * LANES)
        fine_out[span] = (fine_ref[span].astype(F32) + dot(lower, fine)).astype(BF16)
        if j % 2 == 1:
            part = pl.ds((j - 1) * LANES, 2 * LANES)
            copies.append(
                pltpu.make_async_copy(fine_out.at[part], fine_out_hbm.at[part], sems.at[(j + 1) // 2])
            )
            copies[-1].start()
    for copy in copies:
        copy.wait()


def pair_slot():
    return lax.rem(lax.axis_index("wide") + lax.axis_index("core"), 2)


def quad_slot():
    return lax.rem(lax.axis_index("wide") + 2 * lax.axis_index("core"), 4)


def device_of(wide, chip, core):
    sizes = [lax.axis_size(name) for name in ("wide", "chip", "core")]
    return (wide % sizes[0] * sizes[1] + chip) * sizes[2] + core


def exchanged(value, groups):
    return lax.all_to_all(
        value, ("wide", "chip", "core"), 0, 0, tiled=True, axis_index_groups=groups
    )


def core_swapped(value):
    return lax.ppermute(value, "core", [(0, 1), (1, 0)])


def call(kernel, out, scratch=(), vmem=24, hbm=(), hbm_outs=False, nargs=0, flops=0, moved=0):
    specs = [
        pl.BlockSpec(memory_space=pl.ANY if k in hbm else pltpu.VMEM) for k in range(nargs)
    ]
    outs = [jax.ShapeDtypeStruct(shape, dtype) for shape, dtype in out]
    return pl.pallas_call(
        kernel,
        out_shape=outs,
        in_specs=specs,
        out_specs=[pl.BlockSpec(memory_space=pl.ANY if hbm_outs else pltpu.VMEM) for _ in outs],
        scratch_shapes=list(scratch),
        compiler_params=pltpu.CompilerParams(vmem_limit_bytes=vmem * 2**20),
        cost_estimate=pl.CostEstimate(flops=flops, bytes_accessed=moved, transcendentals=0),
    )


def body(
    fine_state, l2_state, l3_state, boundary, senders, receivers, up_parent, l2_parent, msg_in,
    msg_out, fine_gain, up_weight, l2_gain, l3_gain, l3_w1, l3_w2, down_weight, fine_down,
):
    nodes, width = fine_state.shape
    edges = senders.shape[0]
    level_two = l2_state.shape[0]
    level_three = l3_state.shape[0]
    wide = lax.axis_size("wide")
    rows = level_three // wide
    chips, cores = lax.axis_size("chip"), lax.axis_size("core")
    send = senders.reshape(-1, LANES)
    recv = receivers.reshape(-1, LANES)
    par = up_parent.reshape(-1, LANES)
    parent = l2_parent.reshape(-1, LANES)
    fine_gain, l2_gain, l3_gain = (g.reshape(1, width) for g in (fine_gain, l2_gain, l3_gain))

    hot = (boundary[:, None] == jnp.arange(nodes, dtype=jnp.int32)[None, :]).astype(BF16)
    exported = dot(hot, fine_state).astype(BF16)
    bound = chips * cores * boundary.shape[0]
    pairs = [
        [device_of(first + core + step, chip, core) for step in range(2) for chip in range(chips)]
        for core in range(cores)
        for first in range(0, wide, 2)
    ]
    quads = [
        [device_of(first + 2 * core + step, chip, core) for step in range(4)]
        for core in range(cores)
        for chip in range(chips)
        for first in range(0, wide, 4)
    ]

    (chip_rows,) = call(
        chip_rows_kernel, [((2 * chips, cores * boundary.shape[0], width), BF16)], nargs=2,
        flops=6_000_000_000,
    )(exported, core_swapped(exported))
    chip_rows, local_state = lax.optimization_barrier((chip_rows, fine_state))
    pair = exchanged(chip_rows, pairs).reshape(2, bound, width)

    (pre,) = call(
        gather_kernel,
        [((edges, width), BF16)],
        [pltpu.VMEM((2 * nodes, width), BF16), pltpu.VMEM((edges, 2 * nodes), BF16)],
        nargs=4, flops=5_000_000_000, moved=2_000_000,
    )(local_state, msg_in, send, recv)
    pair, pre = lax.optimization_barrier((pair, pre))
    (near,) = call(neighbour_kernel, [((bound, width), BF16)], nargs=1)(pair)
    far = core_swapped(near)
    near, recv_late = lax.optimization_barrier((near, recv))
    (incidence,) = call(
        incidence_kernel, [((nodes, edges), BF16)],
        nargs=1, flops=1_000_000_000, moved=4_000_000,
    )(recv_late)
    far, incidence = lax.optimization_barrier((far, incidence))

    fine_mid, part = call(
        fine_kernel,
        [((nodes, width), BF16), ((level_two, width), BF16)],
        [
            pltpu.VMEM((3 * bound, width), BF16),
            pltpu.VMEM((nodes, width), F32),
            pltpu.VMEM((level_two, nodes), BF16),
            pltpu.VMEM((edges, 3 * bound), BF16),
        ],
        nargs=10, flops=3_000_000_000, moved=4_000_000,
    )(pre, pair, far, fine_state, send, incidence, par, msg_in, msg_out, fine_gain)

    (chip_sums,) = call(add_kernel, [((chips, level_two, width), BF16)], nargs=2)(
        part, core_swapped(part)
    )
    chip_sums = lax.all_to_all(chip_sums, "chip", 0, 0, tiled=True)
    own, pieces, l2_mid, l3_rows = call(
        functools.partial(window_kernel, level_three),
        [
            ((3 * rows, width), F32),
            ((4, 2 * rows, width), BF16),
            ((level_two, width), BF16),
            ((3 * rows, width), BF16),
        ],
        [pltpu.VMEM((7 * rows, width), BF16), pltpu.SemaphoreType.DMA((3,))],
        hbm=(5,), nargs=6,
    )(chip_sums, l2_state, up_weight, l2_gain, parent, l3_state)
    (mine,) = call(
        collect_kernel, [((3 * rows, width), BF16)], [pltpu.VMEM((3 * rows, width), F32)], nargs=1
    )(exchanged(pieces, quads))

    fine_out, l2_down = call(
        functools.partial(down_kernel, level_three),
        [((nodes, width), BF16), ((level_two, width), BF16)],
        [
            pltpu.VMEM((nodes, width), BF16),
            pltpu.VMEM((level_two, width), BF16),
            pltpu.SemaphoreType.DMA((1 + nodes // (2 * LANES),)),
        ],
        nargs=13, hbm_outs=True,
    )(
        own, mine, core_swapped(mine), l3_rows, l3_gain, l3_w1, l3_w2, down_weight, fine_down,
        parent, l2_mid, par, fine_mid,
    )
    return (fine_out, l2_down)


def solution(mesh):
    wide, narrow = mesh.devices.shape
    mesh = jax.sharding.Mesh(mesh.devices.reshape(wide, narrow // 2, 2), ("wide", "chip", "core"))
    every = ("wide", "chip", "core")
    return jax.shard_map(
        body,
        mesh=mesh,
        in_specs=(P(every, None), P("wide", None), P()) + (P(every),) * 4 + (P("wide"),) + (P(),) * 10,
        out_specs=(P(every, None), P("wide", None)),
        check_vma=False,
    )
```

```python
import functools

import jax
import jax.numpy as jnp
from jax import lax
from jax.experimental import pallas as pl
from jax.experimental.pallas import tpu as pltpu
from jax.sharding import PartitionSpec as P

F32 = jnp.float32
BF16 = jnp.bfloat16
LANES = 128
EDGE_BLOCK = 512


def dot(a, b):
    return jnp.dot(a, b, preferred_element_type=F32)


def rms_scale(values, gain):
    return values * lax.rsqrt(jnp.mean(values * values, axis=-1, keepdims=True) + 1e-05) * gain


def silu(x):
    half = 0.5 * x
    return half + half * jnp.tanh(half)


def column_parts(*indices):
    parts = []
    for index in indices:
        parts.append((index & (LANES - 1)).astype(F32))
        parts.append((index >> 7).astype(F32))
    columns = jnp.concatenate(parts, axis=0).T
    out, start = [], 0
    for index in indices:
        k = index.shape[0]
        out.append((columns[:, start : start + k], columns[:, start + k : start + 2 * k]))
        start += 2 * k
    return out


def lane_select(low_col, high_col):
    lane = lax.broadcasted_iota(jnp.int32, (LANES, LANES), 1).astype(F32)
    low = jnp.broadcast_to(low_col, (LANES, LANES))
    hot = jnp.where(low == lane, 1.0, 0.0).astype(BF16)
    high = jnp.broadcast_to(high_col, (LANES, LANES)).astype(BF16)
    return hot, high


def row_select(index_row):
    sub = lax.broadcasted_iota(jnp.int32, (LANES, LANES), 0)
    hot = jnp.where((index_row & (LANES - 1)) == sub, 1.0, 0.0).astype(BF16)
    high = jnp.broadcast_to((index_row >> 7).astype(F32), (LANES, LANES)).astype(BF16)
    return hot, high


def pick(hot, high, tile):
    return jnp.where(high == jnp.asarray(tile, BF16), hot, jnp.zeros_like(hot))


def gather_kernel(fs_ref, w_in_ref, send_ref, recv_ref, pre_ref, proj, hot):
    nodes, width = fs_ref.shape
    edges = pre_ref.shape[0]
    proj[:nodes] = dot(fs_ref[...], w_in_ref[:width]).astype(BF16)
    proj[nodes:] = dot(fs_ref[...], w_in_ref[width:]).astype(BF16)
    columns = column_parts(send_ref[...], recv_ref[...])
    for block in range(edges // EDGE_BLOCK):
        for part in range(EDGE_BLOCK // LANES):
            j = block * (EDGE_BLOCK // LANES) + part
            span = slice(j * LANES, (j + 1) * LANES)
            for side, (low, high) in enumerate(columns):
                hot_j, high_j = lane_select(low[:, j : j + 1], high[:, j : j + 1])
                for t in range(nodes // LANES):
                    start = side * nodes + t * LANES
                    hot[span, start : start + LANES] = pick(hot_j, high_j, t)
        span = slice(block * EDGE_BLOCK, (block + 1) * EDGE_BLOCK)
        pre_ref[span] = dot(hot[span], proj[...]).astype(BF16)


def chip_rows_kernel(mine_ref, other_ref, out_ref):
    rows = mine_ref.shape[0]
    core = lax.axis_index("core")
    first = jnp.where(core == 0, mine_ref[...], other_ref[...])
    last = jnp.where(core == 0, other_ref[...], mine_ref[...])
    for k in range(out_ref.shape[0]):
        out_ref[k, :rows] = first
        out_ref[k, rows:] = last


def neighbour_kernel(pair_ref, out_ref):
    out_ref[...] = pair_ref[1 - pair_slot()]


def incidence_kernel(recv_ref, inc_ref):
    for j in range(recv_ref.shape[0]):
        hot, high = row_select(recv_ref[j : j + 1])
        for t in range(inc_ref.shape[0] // LANES):
            inc_ref[t * LANES : (t + 1) * LANES, j * LANES : (j + 1) * LANES] = pick(hot, high, t)


def fine_kernel(
    pre_ref, pair_ref, far_ref, fs_ref, send_ref, inc_ref, par_ref, w_in_ref, w_out_ref, gain_ref,
    mid_ref, part_ref, around, agg, upper, hot,
):
    nodes, width = fs_ref.shape
    edges = pre_ref.shape[0]
    tiles = nodes // LANES
    bound = far_ref.shape[0]
    slot = pair_slot()
    ahead = lax.rem(lax.axis_index("wide") + lax.axis_index("core"), 2) == 0
    near_at, far_at = jnp.where(ahead, 2 * bound, 0), jnp.where(ahead, 0, 2 * bound)
    around[pl.ds(pl.multiple_of(near_at, bound), bound)] = pair_ref[1 - slot]
    around[bound : 2 * bound] = pair_ref[slot]
    around[pl.ds(pl.multiple_of(far_at, bound), bound)] = far_ref[...]
    proj = dot(around[...], w_in_ref[:width]).astype(BF16)
    ((low, high),) = column_parts(send_ref[...])
    for j in range(tiles):
        hot_p, high_p = row_select(par_ref[j : j + 1])
        for t in range(upper.shape[0] // LANES):
            upper[t * LANES : (t + 1) * LANES, j * LANES : (j + 1) * LANES] = pick(hot_p, high_p, t)
    for block in range(edges // EDGE_BLOCK):
        span = slice(block * EDGE_BLOCK, (block + 1) * EDGE_BLOCK)
        for j in range(block * EDGE_BLOCK // LANES, (block + 1) * EDGE_BLOCK // LANES):
            hot_s, high_s = lane_select(low[:, j : j + 1], high[:, j : j + 1])
            for t in range(hot.shape[1] // LANES):
                hot[j * LANES : (j + 1) * LANES, t * LANES : (t + 1) * LANES] = pick(
                    hot_s, high_s, tiles + t
                )
        hidden = silu(pre_ref[span].astype(F32) + dot(hot[span], proj)).astype(BF16)
        more = dot(inc_ref[:, span], hidden)
        agg[...] = more if block == 0 else agg[...] + more
    for block in range(nodes // EDGE_BLOCK):
        span = slice(block * EDGE_BLOCK, (block + 1) * EDGE_BLOCK)
        summed = dot(agg[span].astype(BF16), w_out_ref[...])
        mid_ref[span] = (fs_ref[span].astype(F32) + rms_scale(summed, gain_ref[...])).astype(BF16)
    part_ref[...] = dot(upper[...], mid_ref[...]).astype(BF16)


def add_kernel(a_ref, b_ref, out_ref):
    total = (a_ref[...].astype(F32) + b_ref[...].astype(F32)).astype(BF16)
    for k in range(out_ref.shape[0]):
        out_ref[k] = total


def coarse_parent(parent_ref, rows, level_three):
    start = (lax.axis_index("wide") - 1) * rows
    local = (parent_ref[...] - start) & (level_three - 1)
    sub = lax.broadcasted_iota(jnp.int32, (3 * rows, LANES), 0)
    return jnp.concatenate(
        [jnp.where(local[j : j + 1] == sub, 1.0, 0.0) for j in range(parent_ref.shape[0])], axis=1
    )


def window_kernel(
    level_three, parts_ref, state_ref, w_up_ref, gain_ref, parent_ref,
    own_ref, pieces_ref, mid_ref, padded,
):
    rows = own_ref.shape[0] // 3
    core = lax.axis_index("core")
    total = parts_ref[0].astype(F32)
    for k in range(1, parts_ref.shape[0]):
        total = total + parts_ref[k].astype(F32)
    level = dot(total.astype(BF16), w_up_ref[...])
    mid = (state_ref[...].astype(F32) + rms_scale(level, gain_ref[...])).astype(BF16)
    mid_ref[...] = mid
    own = dot(coarse_parent(parent_ref, rows, level_three).astype(BF16), mid)
    own_ref[...] = own
    padded[...] = jnp.zeros_like(padded)
    padded[rows : 4 * rows] = own.astype(BF16)
    here = quad_slot()
    for there in range(pieces_ref.shape[0]):
        step = there - here
        start = jnp.where(
            step == 1, 2, jnp.where(step == 2, 3, jnp.where(step == -1, 1, jnp.where(step == -2, 0, 5)))
        )
        start = jnp.where((core == 1) & ((here >= 2) == (there >= 2)), 5, start)
        pieces_ref[there] = padded[pl.ds(pl.multiple_of(start * rows, rows), 2 * rows)]


def collect_kernel(pieces_ref, out_ref, sums):
    rows = out_ref.shape[0] // 3
    sums[...] = jnp.zeros_like(sums)
    here = quad_slot()
    for there in range(pieces_ref.shape[0]):
        start = pl.multiple_of(jnp.where(there < here, 0, rows), rows)
        sums[pl.ds(start, 2 * rows)] += pieces_ref[there].astype(F32)
    out_ref[...] = sums[...].astype(BF16)


def down_kernel(
    level_three, own_ref, mine_ref, other_ref, l3_ref, gain_ref,
    w1_ref, w2_ref, w_down_ref, w_fine_ref, parent_ref, mid_ref, par_ref, fine_ref,
    fine_out_hbm, down_hbm, fine_out, down_out, lower_fine, sems,
):
    rows = own_ref.shape[0] // 3
    total = own_ref[...] + (mine_ref[...].astype(F32) + other_ref[...].astype(F32))
    wide = lax.axis_index("wide")
    count = lax.axis_size("wide")
    state = []
    for k in range(3):
        block = lax.rem(wide + (k + count - 1), count)
        state.append(l3_ref[pl.ds(pl.multiple_of(block * rows, rows), rows)])
    mid3 = (jnp.concatenate(state, axis=0).astype(F32) + rms_scale(total, gain_ref[...])).astype(BF16)
    hidden = silu(dot(mid3, w1_ref[...])).astype(BF16)
    new = (mid3.astype(F32) + dot(hidden, w2_ref[...])).astype(BF16)
    lower = coarse_parent(parent_ref, rows, level_three).T.astype(BF16)
    picked = dot(lower, new).astype(BF16)
    down = (mid_ref[...].astype(F32) + dot(picked, w_down_ref[...])).astype(BF16)
    down_out[...] = down
    copies = [pltpu.make_async_copy(down_out, down_hbm, sems.at[0])]
    copies[0].start()
    fine = dot(down, w_fine_ref[...]).astype(BF16)
    ((par_low, par_high),) = column_parts(par_ref[...])
    for j in range(par_ref.shape[0]):
        hot, high = lane_select(par_low[:, j : j + 1], par_high[:, j : j + 1])
        for t in range(fine.shape[0] // LANES):
            lower_fine[j * LANES : (j + 1) * LANES, t * LANES : (t + 1) * LANES] = pick(hot, high, t)
    for block in range(fine_out.shape[0] // EDGE_BLOCK):
        span = slice(block * EDGE_BLOCK, (block + 1) * EDGE_BLOCK)
        fine_out[span] = (fine_ref[span].astype(F32) + dot(lower_fine[span], fine)).astype(BF16)
        part = pl.ds(block * EDGE_BLOCK, EDGE_BLOCK)
        copies.append(
            pltpu.make_async_copy(fine_out.at[part], fine_out_hbm.at[part], sems.at[block + 1])
        )
        copies[-1].start()
    for copy in copies:
        copy.wait()


def pair_slot():
    return lax.rem(lax.axis_index("wide") + lax.axis_index("core"), 2)


def quad_slot():
    return lax.rem(lax.axis_index("wide") + 2 * lax.axis_index("core"), 4)


def device_of(wide, chip, core):
    sizes = [lax.axis_size(name) for name in ("wide", "chip", "core")]
    return (wide % sizes[0] * sizes[1] + chip) * sizes[2] + core


def exchanged(value, groups):
    return lax.all_to_all(
        value, ("wide", "chip", "core"), 0, 0, tiled=True, axis_index_groups=groups
    )


def core_swapped(value):
    return lax.ppermute(value, "core", [(0, 1), (1, 0)])


def call(kernel, out, scratch=(), vmem=24, hbm=(), hbm_outs=False, nargs=0, flops=0, moved=0):
    specs = [
        pl.BlockSpec(memory_space=pl.ANY if k in hbm else pltpu.VMEM) for k in range(nargs)
    ]
    outs = [jax.ShapeDtypeStruct(shape, dtype) for shape, dtype in out]
    return pl.pallas_call(
        kernel,
        out_shape=outs,
        in_specs=specs,
        out_specs=[pl.BlockSpec(memory_space=pl.ANY if hbm_outs else pltpu.VMEM) for _ in outs],
        scratch_shapes=list(scratch),
        compiler_params=pltpu.CompilerParams(vmem_limit_bytes=vmem * 2**20),
        cost_estimate=pl.CostEstimate(flops=flops, bytes_accessed=moved, transcendentals=0),
    )


def body(
    fine_state, l2_state, l3_state, boundary, senders, receivers, up_parent, l2_parent, msg_in,
    msg_out, fine_gain, up_weight, l2_gain, l3_gain, l3_w1, l3_w2, down_weight, fine_down,
):
    nodes, width = fine_state.shape
    edges = senders.shape[0]
    level_two = l2_state.shape[0]
    level_three = l3_state.shape[0]
    wide = lax.axis_size("wide")
    rows = level_three // wide
    chips, cores = lax.axis_size("chip"), lax.axis_size("core")
    send = senders.reshape(-1, LANES)
    recv = receivers.reshape(-1, LANES)
    par = up_parent.reshape(-1, LANES)
    parent = l2_parent.reshape(-1, LANES)
    fine_gain, l2_gain, l3_gain = (g.reshape(1, width) for g in (fine_gain, l2_gain, l3_gain))

    hot = (boundary[:, None] == jnp.arange(nodes, dtype=jnp.int32)[None, :]).astype(BF16)
    exported = dot(hot, fine_state).astype(BF16)
    bound = chips * cores * boundary.shape[0]
    pairs = [
        [device_of(first + core + step, chip, core) for step in range(2) for chip in range(chips)]
        for core in range(cores)
        for first in range(0, wide, 2)
    ]
    quads = [
        [device_of(first + 2 * core + step, chip, core) for step in range(4)]
        for core in range(cores)
        for chip in range(chips)
        for first in range(0, wide, 4)
    ]

    (chip_rows,) = call(
        chip_rows_kernel, [((2 * chips, cores * boundary.shape[0], width), BF16)], nargs=2,
        flops=6_000_000_000,
    )(exported, core_swapped(exported))
    chip_rows, local_state = lax.optimization_barrier((chip_rows, fine_state))
    pair = exchanged(chip_rows, pairs).reshape(2, bound, width)

    (pre,) = call(
        gather_kernel,
        [((edges, width), BF16)],
        [pltpu.VMEM((2 * nodes, width), BF16), pltpu.VMEM((edges, 2 * nodes), BF16)],
        nargs=4, flops=5_000_000_000, moved=2_000_000,
    )(local_state, msg_in, send, recv)
    pair, pre = lax.optimization_barrier((pair, pre))
    (near,) = call(neighbour_kernel, [((bound, width), BF16)], nargs=1)(pair)
    far = core_swapped(near)
    near, recv_late = lax.optimization_barrier((near, recv))
    (incidence,) = call(
        incidence_kernel, [((nodes, edges), BF16)],
        nargs=1, flops=1_000_000_000, moved=4_000_000,
    )(recv_late)
    far, incidence = lax.optimization_barrier((far, incidence))

    fine_mid, part = call(
        fine_kernel,
        [((nodes, width), BF16), ((level_two, width), BF16)],
        [
            pltpu.VMEM((3 * bound, width), BF16),
            pltpu.VMEM((nodes, width), F32),
            pltpu.VMEM((level_two, nodes), BF16),
            pltpu.VMEM((edges, 3 * bound), BF16),
        ],
        nargs=10, flops=3_000_000_000, moved=4_000_000,
    )(pre, pair, far, fine_state, send, incidence, par, msg_in, msg_out, fine_gain)

    (chip_sums,) = call(add_kernel, [((chips, level_two, width), BF16)], nargs=2)(
        part, core_swapped(part)
    )
    chip_sums = lax.all_to_all(chip_sums, "chip", 0, 0, tiled=True)
    own, pieces, l2_mid = call(
        functools.partial(window_kernel, level_three),
        [
            ((3 * rows, width), F32),
            ((4, 2 * rows, width), BF16),
            ((level_two, width), BF16),
        ],
        [pltpu.VMEM((7 * rows, width), BF16)],
        nargs=5,
    )(chip_sums, l2_state, up_weight, l2_gain, parent)
    (mine,) = call(
        collect_kernel, [((3 * rows, width), BF16)], [pltpu.VMEM((3 * rows, width), F32)], nargs=1
    )(exchanged(pieces, quads))

    fine_out, l2_down = call(
        functools.partial(down_kernel, level_three),
        [((nodes, width), BF16), ((level_two, width), BF16)],
        [
            pltpu.VMEM((nodes, width), BF16),
            pltpu.VMEM((level_two, width), BF16),
            pltpu.VMEM((nodes, level_two), BF16),
            pltpu.SemaphoreType.DMA((1 + nodes // EDGE_BLOCK,)),
        ],
        nargs=13, hbm_outs=True,
    )(
        own, mine, core_swapped(mine), l3_state, l3_gain, l3_w1, l3_w2, down_weight, fine_down,
        parent, l2_mid, par, fine_mid,
    )
    return (fine_out, l2_down)


def solution(mesh):
    wide, narrow = mesh.devices.shape
    mesh = jax.sharding.Mesh(mesh.devices.reshape(wide, narrow // 2, 2), ("wide", "chip", "core"))
    every = ("wide", "chip", "core")
    return jax.shard_map(
        body,
        mesh=mesh,
        in_specs=(P(every, None), P("wide", None), P()) + (P(every),) * 4 + (P("wide"),) + (P(),) * 10,
        out_specs=(P(every, None), P("wide", None)),
        check_vma=False,
    )
```

```python
import functools

import jax
import jax.numpy as jnp
from jax import lax
from jax.experimental import pallas as pl
from jax.experimental.pallas import tpu as pltpu
from jax.sharding import PartitionSpec as P

F32 = jnp.float32
BF16 = jnp.bfloat16
LANES = 128
EDGE_BLOCK = 512
FINE_BLOCK = 1024


def dot(a, b):
    return jnp.dot(a, b, preferred_element_type=F32)


def rms_scale(values, gain):
    return values * lax.rsqrt(jnp.mean(values * values, axis=-1, keepdims=True) + 1e-05) * gain


def silu(x):
    half = 0.5 * x
    return half + half * jnp.tanh(half)


def column_parts(*indices):
    parts = []
    for index in indices:
        parts.append((index & (LANES - 1)).astype(F32))
        parts.append((index >> 7).astype(F32))
    columns = jnp.concatenate(parts, axis=0).T
    out, start = [], 0
    for index in indices:
        k = index.shape[0]
        out.append((columns[:, start : start + k], columns[:, start + k : start + 2 * k]))
        start += 2 * k
    return out


def lane_select(low_col, high_col):
    lane = lax.broadcasted_iota(jnp.int32, (LANES, LANES), 1).astype(F32)
    low = jnp.broadcast_to(low_col, (LANES, LANES))
    hot = jnp.where(low == lane, 1.0, 0.0).astype(BF16)
    high = jnp.broadcast_to(high_col, (LANES, LANES)).astype(BF16)
    return hot, high


def row_select(index_row):
    sub = lax.broadcasted_iota(jnp.int32, (LANES, LANES), 0)
    hot = jnp.where((index_row & (LANES - 1)) == sub, 1.0, 0.0).astype(BF16)
    high = jnp.broadcast_to((index_row >> 7).astype(F32), (LANES, LANES)).astype(BF16)
    return hot, high


def pick(hot, high, tile):
    return jnp.where(high == jnp.asarray(tile, BF16), hot, jnp.zeros_like(hot))


def gather_kernel(fs_ref, w_in_ref, send_ref, recv_ref, pre_ref, proj, hot):
    nodes, width = fs_ref.shape
    edges = pre_ref.shape[0]
    proj[:nodes] = dot(fs_ref[...], w_in_ref[:width]).astype(BF16)
    proj[nodes:] = dot(fs_ref[...], w_in_ref[width:]).astype(BF16)
    columns = column_parts(send_ref[...], recv_ref[...])
    for block in range(edges // EDGE_BLOCK):
        for part in range(EDGE_BLOCK // LANES):
            j = block * (EDGE_BLOCK // LANES) + part
            span = slice(j * LANES, (j + 1) * LANES)
            for side, (low, high) in enumerate(columns):
                hot_j, high_j = lane_select(low[:, j : j + 1], high[:, j : j + 1])
                for t in range(nodes // LANES):
                    start = side * nodes + t * LANES
                    hot[span, start : start + LANES] = pick(hot_j, high_j, t)
        span = slice(block * EDGE_BLOCK, (block + 1) * EDGE_BLOCK)
        pre_ref[span] = dot(hot[span], proj[...]).astype(BF16)


def chip_rows_kernel(mine_ref, other_ref, out_ref):
    rows = mine_ref.shape[0]
    core = lax.axis_index("core")
    first = jnp.where(core == 0, mine_ref[...], other_ref[...])
    last = jnp.where(core == 0, other_ref[...], mine_ref[...])
    for k in range(out_ref.shape[0]):
        out_ref[k, :rows] = first
        out_ref[k, rows:] = last


def neighbour_kernel(pair_ref, out_ref):
    out_ref[...] = pair_ref[1 - pair_slot()]


def incidence_kernel(recv_ref, inc_ref):
    for j in range(recv_ref.shape[0]):
        hot, high = row_select(recv_ref[j : j + 1])
        for t in range(inc_ref.shape[0] // LANES):
            inc_ref[t * LANES : (t + 1) * LANES, j * LANES : (j + 1) * LANES] = pick(hot, high, t)


def fine_kernel(
    pre_ref, pair_ref, far_ref, fs_ref, send_ref, inc_ref, par_ref, w_in_ref, w_out_ref, gain_ref,
    mid_ref, part_ref, around, agg, upper, hot,
):
    nodes, width = fs_ref.shape
    edges = pre_ref.shape[0]
    tiles = nodes // LANES
    bound = far_ref.shape[0]
    slot = pair_slot()
    ahead = lax.rem(lax.axis_index("wide") + lax.axis_index("core"), 2) == 0
    near_at, far_at = jnp.where(ahead, 2 * bound, 0), jnp.where(ahead, 0, 2 * bound)
    around[pl.ds(pl.multiple_of(near_at, bound), bound)] = pair_ref[1 - slot]
    around[bound : 2 * bound] = pair_ref[slot]
    around[pl.ds(pl.multiple_of(far_at, bound), bound)] = far_ref[...]
    proj = dot(around[...], w_in_ref[:width]).astype(BF16)
    ((low, high),) = column_parts(send_ref[...])
    for j in range(tiles):
        hot_p, high_p = row_select(par_ref[j : j + 1])
        for t in range(upper.shape[0] // LANES):
            upper[t * LANES : (t + 1) * LANES, j * LANES : (j + 1) * LANES] = pick(hot_p, high_p, t)
    for block in range(edges // FINE_BLOCK):
        span = slice(block * FINE_BLOCK, (block + 1) * FINE_BLOCK)
        for j in range(block * FINE_BLOCK // LANES, (block + 1) * FINE_BLOCK // LANES):
            hot_s, high_s = lane_select(low[:, j : j + 1], high[:, j : j + 1])
            for t in range(hot.shape[1] // LANES):
                hot[j * LANES : (j + 1) * LANES, t * LANES : (t + 1) * LANES] = pick(
                    hot_s, high_s, tiles + t
                )
        hidden = silu(pre_ref[span].astype(F32) + dot(hot[span], proj)).astype(BF16)
        more = dot(inc_ref[:, span], hidden)
        agg[...] = more if block == 0 else agg[...] + more
    for block in range(nodes // EDGE_BLOCK):
        span = slice(block * EDGE_BLOCK, (block + 1) * EDGE_BLOCK)
        summed = dot(agg[span].astype(BF16), w_out_ref[...])
        mid_ref[span] = (fs_ref[span].astype(F32) + rms_scale(summed, gain_ref[...])).astype(BF16)
    part_ref[...] = dot(upper[...], mid_ref[...]).astype(BF16)


def add_kernel(a_ref, b_ref, out_ref):
    total = (a_ref[...].astype(F32) + b_ref[...].astype(F32)).astype(BF16)
    for k in range(out_ref.shape[0]):
        out_ref[k] = total


def coarse_parent(parent_ref, rows, level_three):
    start = (lax.axis_index("wide") - 1) * rows
    local = (parent_ref[...] - start) & (level_three - 1)
    sub = lax.broadcasted_iota(jnp.int32, (3 * rows, LANES), 0)
    return jnp.concatenate(
        [jnp.where(local[j : j + 1] == sub, 1.0, 0.0) for j in range(parent_ref.shape[0])], axis=1
    )


def window_kernel(
    level_three, parts_ref, state_ref, w_up_ref, gain_ref, parent_ref,
    own_ref, pieces_ref, mid_ref, padded,
):
    rows = own_ref.shape[0] // 3
    core = lax.axis_index("core")
    total = parts_ref[0].astype(F32)
    for k in range(1, parts_ref.shape[0]):
        total = total + parts_ref[k].astype(F32)
    level = dot(total.astype(BF16), w_up_ref[...])
    mid = (state_ref[...].astype(F32) + rms_scale(level, gain_ref[...])).astype(BF16)
    mid_ref[...] = mid
    own = dot(coarse_parent(parent_ref, rows, level_three).astype(BF16), mid)
    own_ref[...] = own
    padded[...] = jnp.zeros_like(padded)
    padded[rows : 4 * rows] = own.astype(BF16)
    here = quad_slot()
    for there in range(pieces_ref.shape[0]):
        step = there - here
        start = jnp.where(
            step == 1, 2, jnp.where(step == 2, 3, jnp.where(step == -1, 1, jnp.where(step == -2, 0, 5)))
        )
        start = jnp.where((core == 1) & ((here >= 2) == (there >= 2)), 5, start)
        pieces_ref[there] = padded[pl.ds(pl.multiple_of(start * rows, rows), 2 * rows)]


def collect_kernel(pieces_ref, out_ref, sums):
    rows = out_ref.shape[0] // 3
    sums[...] = jnp.zeros_like(sums)
    here = quad_slot()
    for there in range(pieces_ref.shape[0]):
        start = pl.multiple_of(jnp.where(there < here, 0, rows), rows)
        sums[pl.ds(start, 2 * rows)] += pieces_ref[there].astype(F32)
    out_ref[...] = sums[...].astype(BF16)


def down_kernel(
    level_three, own_ref, mine_ref, other_ref, l3_ref, gain_ref,
    w1_ref, w2_ref, w_down_ref, w_fine_ref, parent_ref, mid_ref, par_ref, fine_ref,
    fine_out_hbm, down_hbm, fine_out, down_out, lower_fine, sems,
):
    rows = own_ref.shape[0] // 3
    total = own_ref[...] + (mine_ref[...].astype(F32) + other_ref[...].astype(F32))
    wide = lax.axis_index("wide")
    count = lax.axis_size("wide")
    state = []
    for k in range(3):
        block = lax.rem(wide + (k + count - 1), count)
        state.append(l3_ref[pl.ds(pl.multiple_of(block * rows, rows), rows)])
    mid3 = (jnp.concatenate(state, axis=0).astype(F32) + rms_scale(total, gain_ref[...])).astype(BF16)
    hidden = silu(dot(mid3, w1_ref[...])).astype(BF16)
    new = (mid3.astype(F32) + dot(hidden, w2_ref[...])).astype(BF16)
    lower = coarse_parent(parent_ref, rows, level_three).T.astype(BF16)
    picked = dot(lower, new).astype(BF16)
    down = (mid_ref[...].astype(F32) + dot(picked, w_down_ref[...])).astype(BF16)
    down_out[...] = down
    copies = [pltpu.make_async_copy(down_out, down_hbm, sems.at[0])]
    copies[0].start()
    fine = dot(down, w_fine_ref[...]).astype(BF16)
    ((par_low, par_high),) = column_parts(par_ref[...])
    for j in range(par_ref.shape[0]):
        hot, high = lane_select(par_low[:, j : j + 1], par_high[:, j : j + 1])
        for t in range(fine.shape[0] // LANES):
            lower_fine[j * LANES : (j + 1) * LANES, t * LANES : (t + 1) * LANES] = pick(hot, high, t)
    for block in range(fine_out.shape[0] // EDGE_BLOCK):
        span = slice(block * EDGE_BLOCK, (block + 1) * EDGE_BLOCK)
        fine_out[span] = (fine_ref[span].astype(F32) + dot(lower_fine[span], fine)).astype(BF16)
        part = pl.ds(block * EDGE_BLOCK, EDGE_BLOCK)
        copies.append(
            pltpu.make_async_copy(fine_out.at[part], fine_out_hbm.at[part], sems.at[block + 1])
        )
        copies[-1].start()
    for copy in copies:
        copy.wait()


def pair_slot():
    return lax.rem(lax.axis_index("wide") + lax.axis_index("core"), 2)


def quad_slot():
    return lax.rem(lax.axis_index("wide") + 2 * lax.axis_index("core"), 4)


def device_of(wide, chip, core):
    sizes = [lax.axis_size(name) for name in ("wide", "chip", "core")]
    return (wide % sizes[0] * sizes[1] + chip) * sizes[2] + core


def exchanged(value, groups):
    return lax.all_to_all(
        value, ("wide", "chip", "core"), 0, 0, tiled=True, axis_index_groups=groups
    )


def core_swapped(value):
    return lax.ppermute(value, "core", [(0, 1), (1, 0)])


def call(kernel, out, scratch=(), vmem=24, hbm=(), hbm_outs=False, nargs=0, flops=0, moved=0):
    specs = [
        pl.BlockSpec(memory_space=pl.ANY if k in hbm else pltpu.VMEM) for k in range(nargs)
    ]
    outs = [jax.ShapeDtypeStruct(shape, dtype) for shape, dtype in out]
    return pl.pallas_call(
        kernel,
        out_shape=outs,
        in_specs=specs,
        out_specs=[pl.BlockSpec(memory_space=pl.ANY if hbm_outs else pltpu.VMEM) for _ in outs],
        scratch_shapes=list(scratch),
        compiler_params=pltpu.CompilerParams(vmem_limit_bytes=vmem * 2**20),
        cost_estimate=pl.CostEstimate(flops=flops, bytes_accessed=moved, transcendentals=0),
    )


def body(
    fine_state, l2_state, l3_state, boundary, senders, receivers, up_parent, l2_parent, msg_in,
    msg_out, fine_gain, up_weight, l2_gain, l3_gain, l3_w1, l3_w2, down_weight, fine_down,
):
    nodes, width = fine_state.shape
    edges = senders.shape[0]
    level_two = l2_state.shape[0]
    level_three = l3_state.shape[0]
    wide = lax.axis_size("wide")
    rows = level_three // wide
    chips, cores = lax.axis_size("chip"), lax.axis_size("core")
    send = senders.reshape(-1, LANES)
    recv = receivers.reshape(-1, LANES)
    par = up_parent.reshape(-1, LANES)
    parent = l2_parent.reshape(-1, LANES)
    fine_gain, l2_gain, l3_gain = (g.reshape(1, width) for g in (fine_gain, l2_gain, l3_gain))

    hot = (boundary[:, None] == jnp.arange(nodes, dtype=jnp.int32)[None, :]).astype(BF16)
    exported = dot(hot, fine_state).astype(BF16)
    bound = chips * cores * boundary.shape[0]
    pairs = [
        [device_of(first + core + step, chip, core) for step in range(2) for chip in range(chips)]
        for core in range(cores)
        for first in range(0, wide, 2)
    ]
    quads = [
        [device_of(first + 2 * core + step, chip, core) for step in range(4)]
        for core in range(cores)
        for chip in range(chips)
        for first in range(0, wide, 4)
    ]

    (chip_rows,) = call(
        chip_rows_kernel, [((2 * chips, cores * boundary.shape[0], width), BF16)], nargs=2,
        flops=6_000_000_000,
    )(exported, core_swapped(exported))
    chip_rows, local_state = lax.optimization_barrier((chip_rows, fine_state))
    pair = exchanged(chip_rows, pairs).reshape(2, bound, width)

    (pre,) = call(
        gather_kernel,
        [((edges, width), BF16)],
        [pltpu.VMEM((2 * nodes, width), BF16), pltpu.VMEM((edges, 2 * nodes), BF16)],
        nargs=4, flops=5_000_000_000, moved=2_000_000,
    )(local_state, msg_in, send, recv)
    pair, pre = lax.optimization_barrier((pair, pre))
    (near,) = call(neighbour_kernel, [((bound, width), BF16)], nargs=1)(pair)
    far = core_swapped(near)
    near, recv_late = lax.optimization_barrier((near, recv))
    (incidence,) = call(
        incidence_kernel, [((nodes, edges), BF16)],
        nargs=1, flops=1_000_000_000, moved=4_000_000,
    )(recv_late)
    far, incidence = lax.optimization_barrier((far, incidence))

    fine_mid, part = call(
        fine_kernel,
        [((nodes, width), BF16), ((level_two, width), BF16)],
        [
            pltpu.VMEM((3 * bound, width), BF16),
            pltpu.VMEM((nodes, width), F32),
            pltpu.VMEM((level_two, nodes), BF16),
            pltpu.VMEM((edges, 3 * bound), BF16),
        ],
        nargs=10, flops=3_000_000_000, moved=4_000_000,
    )(pre, pair, far, fine_state, send, incidence, par, msg_in, msg_out, fine_gain)

    (chip_sums,) = call(add_kernel, [((chips, level_two, width), BF16)], nargs=2)(
        part, core_swapped(part)
    )
    chip_sums = lax.all_to_all(chip_sums, "chip", 0, 0, tiled=True)
    own, pieces, l2_mid = call(
        functools.partial(window_kernel, level_three),
        [
            ((3 * rows, width), F32),
            ((4, 2 * rows, width), BF16),
            ((level_two, width), BF16),
        ],
        [pltpu.VMEM((7 * rows, width), BF16)],
        nargs=5,
    )(chip_sums, l2_state, up_weight, l2_gain, parent)
    (mine,) = call(
        collect_kernel, [((3 * rows, width), BF16)], [pltpu.VMEM((3 * rows, width), F32)], nargs=1
    )(exchanged(pieces, quads))

    fine_out, l2_down = call(
        functools.partial(down_kernel, level_three),
        [((nodes, width), BF16), ((level_two, width), BF16)],
        [
            pltpu.VMEM((nodes, width), BF16),
            pltpu.VMEM((level_two, width), BF16),
            pltpu.VMEM((nodes, level_two), BF16),
            pltpu.SemaphoreType.DMA((1 + nodes // EDGE_BLOCK,)),
        ],
        nargs=13, hbm_outs=True,
    )(
        own, mine, core_swapped(mine), l3_state, l3_gain, l3_w1, l3_w2, down_weight, fine_down,
        parent, l2_mid, par, fine_mid,
    )
    return (fine_out, l2_down)


def solution(mesh):
    wide, narrow = mesh.devices.shape
    mesh = jax.sharding.Mesh(mesh.devices.reshape(wide, narrow // 2, 2), ("wide", "chip", "core"))
    every = ("wide", "chip", "core")
    return jax.shard_map(
        body,
        mesh=mesh,
        in_specs=(P(every, None), P("wide", None), P()) + (P(every),) * 4 + (P("wide"),) + (P(),) * 10,
        out_specs=(P(every, None), P("wide", None)),
        check_vma=False,
    )
```
